32 devices in a mesh: gx: 8 (over z, x), gy: 2 (over core), gz: 2 (over y).
Axes of the slice: x: 2, y: 2, z: 4, core: 2. Of those that a mesh axis runs over, the one named last changes fastest.
Arguments:
- tokens: bfloat16 [64, 32, 32, 192], P('gx', 'gy', 'gz'), may hold values from -6 to 6
- upstream: bfloat16 [64, 32, 32, 192], P('gx', 'gy', 'gz'), may hold values from -6 to 6
- norm_gain: float32 [192], replicated, may hold values from 0.25 to 1.75
- norm_bias: float32 [192], replicated, may hold values from -3 to 3
- qkv_weight: bfloat16 [192, 576], replicated, may hold values from -4 to 4, as said below
- qkv_bias: float32 [576], replicated, may hold values from -3 to 3
- proj_weight: bfloat16 [192, 192], replicated, may hold values from -0.4375 to 0.4375
Outputs:
- token_grad: bfloat16 [64, 32, 32, 192], P('gx', 'gy', 'gz')
- qkv_weight_grad: float32 [192, 576], replicated
- qkv_bias_grad: float32 [576], replicated
- proj_weight_grad: float32 [192, 192], replicated
- proj_bias_grad: float32 [192], replicated
- gain_grad: float32 [192], replicated
- norm_bias_grad: float32 [192], replicated
The draws below stay inside these ranges and needn't reach their ends.
Inputs may be any that keep to these rules, and one draw needn't show every extreme that they name: `qkv_weight`: columns are the query, key and value projections in that order, each 6 heads of 32 columns.
All inputs are finite; a program needn't handle non-finite values.
Results may differ from the reference program's by a relative error of at most 0.02.
The reference program's roundings to bfloat16 on the way (of `hidden`, `packed`, `probs_half`, `attended`, `attended_grad`, `score_grad` and `packed_grad`) count: a program that leaves them out, or rounds other values in their place, can miss the bound.
Values may be sent and summed in bfloat16 or wider, within the bound.
A program may use at most 64 MiB of HBM per device.

```python
import jax
import jax.numpy as jnp
from jax import lax

C = 192
HEADS = 6
HEAD_DIM = 32
WIN = 8
SHIFT = 4
NX = 64
NY = 32
NZ = 32
TOKENS = 65536


def draw_qkv_weight(key, part):
    base = jax.random.normal(key, (C, 3 * C), jnp.float32) * C ** (-0.5)
    return jnp.clip(base, -4.0, 4.0).astype(jnp.bfloat16)


def spiked(entries, own_key, source, target, blocks, factor):
    owner, partner = [(jnp.arange(entries.shape[dim]) // (entries.shape[dim] // blocks)).reshape([-1 if axis == dim else 1 for axis in range(entries.ndim)]) for dim in (source, target)]
    chosen = jax.random.permutation(own_key, blocks)[partner]
    strong = (owner == chosen) | (owner == (partner + blocks // 2) % blocks)
    return jnp.where(strong, factor * entries, entries)


def block_scale(own_key, dims, pieces, low, largest):
    def one(position, blocks):
        steps = jax.random.uniform(jax.random.fold_in(jax.random.fold_in(own_key, 6), position), (blocks,), jnp.float32, low / len(pieces), largest / len(pieces))
        return jnp.repeat(jnp.exp(steps), dims[position] // blocks).reshape((-1,) + (1,) * (len(dims) - position - 1))

    level = one(*pieces[0])
    for cut in pieces[1:]:
        level = level * one(*cut)
    return level


def gaussian(own_key, dims, scale, most, split=(), kind=jnp.bfloat16):
    drawn = scale * jax.random.normal(own_key, dims, jnp.float32)
    if split:
        drawn = drawn * block_scale(own_key, dims, split, -0.22, 0.18)
    return jnp.clip(drawn, -most, most).astype(kind)


def heavy_noise(key, dims, scale, limit, pieces, heavy, held_as=jnp.bfloat16):
    entries = scale * jax.random.normal(key, dims, jnp.float32)
    if pieces:
        entries = entries * block_scale(key, dims, pieces, -0.22, 0.18)
    return jnp.clip(spiked(entries, jax.random.fold_in(key, 3), *heavy), -limit, limit).astype(held_as)


def setup_inputs(seed: int = 0) -> dict:
    streams_of = jax.random.split(jax.random.key(seed), 8)
    return {
        "tokens": gaussian(streams_of[0], (NX, NY, NZ, C), 1.0, 6.0, ((0, 8), (1, 2), (2, 2))),
        "upstream": heavy_noise(streams_of[1], (NX, NY, NZ, C), 1.0, 6.0, ((0, 8), (1, 2), (2, 2)), (0, 3, 8, 2.0)),
        "norm_gain": jnp.clip(1.0 + 0.15 * jax.random.normal(streams_of[2], (C,), jnp.float32), 0.25, 1.75),
        "norm_bias": gaussian(streams_of[3], (C,), 0.5, 3.0, (), jnp.float32),
        "qkv_weight": draw_qkv_weight(jax.random.fold_in(streams_of[7], 71), 0),
        "qkv_bias": gaussian(streams_of[5], (3 * C,), 0.5, 3.0, (), jnp.float32),
        "proj_weight": gaussian(streams_of[6], (C, C), C ** -0.5, 0.4375),
    }


def window_grads(tok, upward, idents, norm_gain, norm_bias, qkv_weight, qkv_bias, proj_weight):
    length = tok.shape[0]
    width = tok.shape[1]
    single = jnp.float32
    factor = HEAD_DIM ** (-0.5)
    inputs = tok.astype(single)
    centred = inputs - lax.optimization_barrier(jnp.mean(inputs, axis=-1, keepdims=True))
    inverse = lax.rsqrt(lax.optimization_barrier(jnp.mean(centred * centred, axis=-1, keepdims=True)) + 1e-05)
    normed = centred * inverse
    hidden = (normed * norm_gain + norm_bias).astype(jnp.bfloat16)
    packed = (jnp.dot(hidden, qkv_weight, preferred_element_type=single) + qkv_bias).astype(jnp.bfloat16)
    query = packed[:, :width].reshape(length, HEADS, HEAD_DIM).astype(single)
    keyset = packed[:, width:2 * width].reshape(length, HEADS, HEAD_DIM).astype(single)
    valset = packed[:, 2 * width:].reshape(length, HEADS, HEAD_DIM).astype(single)
    scores = jnp.einsum('qhd,khd->hqk', query, keyset) * factor
    same = idents[:, None] == idents[None, :]
    scores = jnp.where(same[None], scores, -1e+30)
    peak = lax.optimization_barrier(jnp.max(scores, axis=-1, keepdims=True))
    expo = jnp.exp(scores - peak)
    probs = expo / lax.optimization_barrier(jnp.sum(expo, axis=-1, keepdims=True))
    probs_half = probs.astype(jnp.bfloat16)
    attended = jnp.einsum('hqk,khd->qhd', probs_half.astype(single), valset).reshape(length, width).astype(jnp.bfloat16)
    up_single = upward.astype(single)
    grad_proj = jnp.dot(attended.T, upward, preferred_element_type=single)
    grad_pbias = lax.optimization_barrier(jnp.sum(up_single, axis=0))
    attended_grad = jnp.dot(upward, proj_weight.T, preferred_element_type=single).astype(jnp.bfloat16)
    attended_grad = attended_grad.reshape(length, HEADS, HEAD_DIM).astype(single)
    prob_grad = jnp.einsum('qhd,khd->hqk', attended_grad, valset)
    inner = lax.optimization_barrier(jnp.sum(probs * prob_grad, axis=-1, keepdims=True))
    score_grad = (probs * (prob_grad - inner) * factor).astype(jnp.bfloat16).astype(single)
    query_grad = jnp.einsum('hqk,khd->qhd', score_grad, keyset).reshape(length, width)
    key_grad = jnp.einsum('hqk,qhd->khd', score_grad, query).reshape(length, width)
    value_grad = jnp.einsum('hqk,qhd->khd', probs_half.astype(single), attended_grad).reshape(length, width)
    packed_grad = jnp.concatenate([query_grad, key_grad, value_grad], axis=1).astype(jnp.bfloat16)
    grad_qkv = jnp.dot(hidden.T, packed_grad, preferred_element_type=single)
    grad_qbias = lax.optimization_barrier(jnp.sum(packed_grad.astype(single), axis=0))
    hidden_grad = jnp.dot(packed_grad, qkv_weight.T, preferred_element_type=single)
    grad_gain = lax.optimization_barrier(jnp.sum(hidden_grad * normed, axis=0))
    grad_nbias = lax.optimization_barrier(jnp.sum(hidden_grad, axis=0))
    normed_grad = hidden_grad * norm_gain
    first = lax.optimization_barrier(jnp.mean(normed_grad, axis=-1, keepdims=True))
    second = lax.optimization_barrier(jnp.mean(normed_grad * normed, axis=-1, keepdims=True))
    token_grad = (up_single + inverse * (normed_grad - first - normed * second)).astype(jnp.bfloat16)
    return (token_grad, (grad_qkv, grad_qbias, grad_proj, grad_pbias, grad_gain, grad_nbias))

def to_windows(block):
    sizes = block.shape[:3]
    rest = block.shape[3:]
    shaped = block.reshape((sizes[0] // WIN, WIN, sizes[1] // WIN, WIN, sizes[2] // WIN, WIN) + rest)
    order = (0, 2, 4, 1, 3, 5) + tuple(range(6, 6 + len(rest)))
    return shaped.transpose(order).reshape((-1, WIN ** 3) + rest)

def from_windows(wins, first, second, third):
    rest = wins.shape[2:]
    shaped = wins.reshape((first // WIN, second // WIN, third // WIN, WIN, WIN, WIN) + rest)
    order = (0, 3, 1, 4, 2, 5) + tuple(range(6, 6 + len(rest)))
    return shaped.transpose(order).reshape((first, second, third) + rest)

def window_index(total):
    placed = (jnp.arange(total, dtype=jnp.int32) + SHIFT) % total
    return ((placed + SHIFT) // WIN, total // WIN + 1)

def reference(tokens, upstream, norm_gain, norm_bias, qkv_weight, qkv_bias, proj_weight):
    rolled = jnp.roll(tokens, (-SHIFT, -SHIFT, -SHIFT), axis=(0, 1, 2))
    rolled_up = jnp.roll(upstream, (-SHIFT, -SHIFT, -SHIFT), axis=(0, 1, 2))
    index_x, span_x = window_index(NX)
    index_y, span_y = window_index(NY)
    index_z, span_z = window_index(NZ)
    idents = (index_x[:, None, None] * span_y + index_y[None, :, None]) * span_z + index_z[None, None, :]
    token_wins = to_windows(rolled)
    up_wins = to_windows(rolled_up)
    ident_wins = to_windows(idents.astype(jnp.int32))
    width = tokens.shape[3]
    zeros = (jnp.zeros((width, 3 * width), jnp.float32), jnp.zeros((3 * width,), jnp.float32), jnp.zeros((width, width), jnp.float32), jnp.zeros((width,), jnp.float32), jnp.zeros((width,), jnp.float32), jnp.zeros((width,), jnp.float32))

    def advance(carry, item):
        grad_win, parts = window_grads(item[0], item[1], item[2], norm_gain, norm_bias, qkv_weight, qkv_bias, proj_weight)
        return (tuple((old + new for old, new in zip(carry, parts))), grad_win)
    totals, grad_wins = lax.scan(advance, zeros, (token_wins, up_wins, ident_wins))
    token_grad = from_windows(grad_wins, NX, NY, NZ)
    factor = float(TOKENS) ** (-0.5)
    return (token_grad, totals[0] * factor, totals[1] * factor, totals[2] * factor, totals[3] * factor, totals[4] * factor, totals[5] * factor)
```

```python
import functools

import jax
import jax.numpy as jnp
from jax import lax
from jax.experimental import pallas as pl
from jax.experimental.pallas import tpu as pltpu
from jax.sharding import PartitionSpec as P

HEADS = 6
WIN = 8
SHIFT = 4
CELL = SHIFT**3
LANES = 128
MASKED = -1e30
MESH = pl.DeviceIdType.MESH


def halo_kernel(counts, cells_ref, wins_ref, send_sem, recv_sem, local_sem):
    axes = ("gx", "gy", "gz")
    here = [lax.axis_index(axis) for axis in axes]
    sizes = [lax.axis_size(axis) for axis in axes]
    offsets = [(i, j, k) for i in (0, 1) for j in (0, 1) for k in (0, 1)]

    def device(offset, sign):
        return {
            axis: lax.rem(at + sign * step + size, size)
            for axis, at, step, size in zip(axes, here, offset, sizes)
        }

    barrier = pltpu.get_barrier_semaphore()
    for offset in offsets[1:]:
        pl.semaphore_signal(barrier, inc=1, device_id=device(offset, 1), device_id_type=MESH)
    pl.semaphore_wait(barrier, len(offsets) - 1)

    spread = [count // 2 for count in counts]
    copies = []
    number = 0
    for a in range(counts[0]):
        for b in range(counts[1]):
            for c in range(counts[2]):
                offset = tuple(int(at == 0) for at in (a, b, c))
                to = [(at - 1) % count for at, count in zip((a, b, c), counts)]
                window = (to[0] // 2 * spread[1] + to[1] // 2) * spread[2] + to[2] // 2
                octant = (to[0] % 2 * 2 + to[1] % 2) * 2 + to[2] % 2
                source = cells_ref.at[a, b, c]
                target = wins_ref.at[window, octant]
                if any(offset):
                    copy = pltpu.make_async_remote_copy(
                        src_ref=source,
                        dst_ref=target,
                        send_sem=send_sem.at[number],
                        recv_sem=recv_sem.at[number],
                        device_id=device(offset, -1),
                        device_id_type=MESH,
                    )
                else:
                    copy = pltpu.make_async_copy(source, target, local_sem.at[number])
                copies.append(copy)
                copy.start()
                number += 1
    for copy in copies:
        copy.wait()


def halo(cells):
    counts = cells.shape[:3]
    total = counts[0] * counts[1] * counts[2]
    return pl.pallas_call(
        functools.partial(halo_kernel, counts),
        out_shape=jax.ShapeDtypeStruct((total // 8, 8) + cells.shape[3:], cells.dtype),
        in_specs=[pl.BlockSpec(memory_space=pl.ANY)],
        out_specs=pl.BlockSpec(memory_space=pl.ANY),
        scratch_shapes=[pltpu.SemaphoreType.DMA((total,))] * 3,
        compiler_params=pltpu.CompilerParams(collective_id=0, has_side_effects=True),
    )(cells)


def dot(left, right):
    return jnp.dot(left, right, preferred_element_type=jnp.float32)


def dot_nt(left, right):
    return lax.dot_general(
        left, right, (((1,), (1,)), ((), ())), preferred_element_type=jnp.float32
    )


def window_kernel(
    spread, width, win_ref, gain_ref, nbias_ref, wt_ref, w_ref, qbias_ref, pw_ref,
    out_ref, g_ref,
    hid_ref, normed_ref, inv_ref, pk_ref, da_ref, att_ref, pg_ref, accq_ref, accp_ref, accs_ref,
):
    step = pl.program_id(0)
    length = WIN**3
    head = width // HEADS
    factor = head ** (-0.5)
    single = jnp.float32
    half = jnp.bfloat16

    @pl.when(step == 0)
    def _():
        hid_ref[...] = jnp.ones_like(hid_ref)
        accq_ref[...] = jnp.zeros_like(accq_ref)
        accp_ref[...] = jnp.zeros_like(accp_ref)
        accs_ref[...] = jnp.zeros_like(accs_ref)

    both = win_ref[0].reshape(length, 2 * width)
    inputs = both[:, :width].astype(single)
    up = both[:, width:]
    centred = inputs - jnp.mean(inputs, axis=-1, keepdims=True)
    inverse = lax.rsqrt(jnp.mean(centred * centred, axis=-1, keepdims=True) + 1e-05)
    normed = centred * inverse
    normed_ref[...] = normed
    inv_ref[...] = inverse
    hidden = (normed * gain_ref[...] + nbias_ref[...]).astype(half)
    hid_ref[:, :width] = hidden
    pk_ref[...] = (dot_nt(wt_ref[...], hidden) + qbias_ref[...]).astype(half)
    da_ref[...] = dot_nt(pw_ref[...], up).astype(half)

    place = (step // (spread[1] * spread[2]), step // spread[2] % spread[1], step % spread[2])
    cut = [
        jnp.where((lax.axis_index(axis) == lax.axis_size(axis) - 1) & (at == count - 1), 1, 0)
        for axis, at, count in zip(("gx", "gy", "gz"), place, spread)
    ]
    octant = lax.broadcasted_iota(jnp.int32, (16, length), 1) // CELL
    region = octant & (cut[0] * 4 + cut[1] * 2 + cut[2])
    own = region == lax.broadcasted_iota(jnp.int32, (16, length), 0)
    mark_q = jnp.where(own, 1.0, 0.0).astype(half)
    mark_k = jnp.where(own, 0.0, MASKED).astype(half)

    tile = min(256, length)
    scale = factor * 1.4426950408889634

    def one_head(h, carry):
        base = pl.multiple_of(h * head, head)
        qt = pk_ref[pl.ds(base, head), :]
        kt = pk_ref[pl.ds(base + width, head), :]
        vt = pk_ref[pl.ds(base + 2 * width, head), :]
        dat = da_ref[pl.ds(base, head), :]
        qt_marked = jnp.concatenate([qt, mark_q], axis=0)
        keys = jnp.concatenate([kt, mark_k], axis=0).T
        values = vt.T
        kg = jnp.zeros((head, length), single)
        vg = jnp.zeros((head, length), single)
        for start in range(0, length, tile):
            part = slice(start, start + tile)
            scores = dot(keys, qt_marked[:, part])
            prob_grad = dot(values, dat[:, part])
            peak = jnp.max(scores, axis=0, keepdims=True)
            expo = jnp.exp2((scores - peak) * scale)
            probs = expo * (1.0 / jnp.sum(expo, axis=0, keepdims=True))
            inner = jnp.sum(probs * prob_grad, axis=0, keepdims=True)
            probs_half = probs.astype(half)
            score_grad = (probs * (prob_grad - inner)).astype(half)
            att_ref[pl.ds(base, head), part] = dot(vt, probs_half).astype(half)
            pg_ref[pl.ds(base, head), part] = (dot(kt, score_grad) * factor).astype(half)
            vg += dot_nt(dat[:, part], probs_half)
            kg += dot_nt(qt[:, part], score_grad)
        pg_ref[pl.ds(base + width, head), :] = (kg * factor).astype(half)
        pg_ref[pl.ds(base + 2 * width, head), :] = vg.astype(half)
        return carry

    lax.fori_loop(0, HEADS, one_head, 0)

    accq_ref[...] += dot(pg_ref[...], hid_ref[...])
    accp_ref[...] += dot(att_ref[...], up)
    hidden_grad = dot(w_ref[...], pg_ref[...]).T
    normed = normed_ref[...]
    inverse = inv_ref[...]
    up_single = up.astype(single)
    accs_ref[0:1, :] += jnp.sum(up_single, axis=0, keepdims=True)
    accs_ref[1:2, :] += jnp.sum(hidden_grad * normed, axis=0, keepdims=True)
    accs_ref[2:3, :] += jnp.sum(hidden_grad, axis=0, keepdims=True)
    normed_grad = hidden_grad * gain_ref[...]
    first = jnp.mean(normed_grad, axis=-1, keepdims=True)
    second = jnp.mean(normed_grad * normed, axis=-1, keepdims=True)
    out_ref[0] = (up_single + inverse * (normed_grad - first - normed * second)).astype(half)

    @pl.when(step == pl.num_programs(0) - 1)
    def _():
        rest = width - LANES
        both_rows = 4 * width
        if g_ref.shape[0] > 2 * both_rows:
            g_ref[2 * both_rows :, :] = jnp.zeros((g_ref.shape[0] - 2 * both_rows, LANES), single)
        g_ref[: 3 * width, :] = accq_ref[:, :LANES]
        g_ref[3 * width : both_rows, :] = accp_ref[:, :LANES]
        g_ref[both_rows : both_rows + 3 * width, :] = accq_ref[:, LANES:]
        last = slice(both_rows + 3 * width, 2 * both_rows)
        g_ref[last, :] = jnp.zeros((width, LANES), single)
        g_ref[last, :rest] = accp_ref[:, LANES:]
        g_ref[last, rest : rest + 8] = accs_ref[...].T


def windows(wins, spread, rows, norm_gain, norm_bias, qkv_weight, qkv_bias, proj_weight):
    count = wins.shape[0]
    width = norm_gain.shape[0]
    length = WIN**3

    def whole(*dims):
        return pl.BlockSpec(dims, lambda i: (0,) * len(dims))

    return pl.pallas_call(
        functools.partial(window_kernel, spread, width),
        grid=(count,),
        out_shape=(
            jax.ShapeDtypeStruct((count, length, width), jnp.bfloat16),
            jax.ShapeDtypeStruct((rows, LANES), jnp.float32),
        ),
        in_specs=[
            pl.BlockSpec((1, 8, CELL, 2 * width), lambda i: (i, 0, 0, 0)),
            whole(1, width),
            whole(1, width),
            whole(3 * width, width),
            whole(width, 3 * width),
            whole(3 * width, 1),
            whole(width, width),
        ],
        out_specs=(pl.BlockSpec((1, length, width), lambda i: (i, 0, 0)), whole(rows, LANES)),
        scratch_shapes=[
            pltpu.VMEM((length, 2 * LANES), jnp.bfloat16),
            pltpu.VMEM((length, width), jnp.float32),
            pltpu.VMEM((length, 1), jnp.float32),
            pltpu.VMEM((3 * width, length), jnp.bfloat16),
            pltpu.VMEM((width, length), jnp.bfloat16),
            pltpu.VMEM((width, length), jnp.bfloat16),
            pltpu.VMEM((3 * width, length), jnp.bfloat16),
            pltpu.VMEM((3 * width, 2 * LANES), jnp.float32),
            pltpu.VMEM((width, width), jnp.float32),
            pltpu.VMEM((8, width), jnp.float32),
        ],
        compiler_params=pltpu.CompilerParams(vmem_limit_bytes=40 * 1024 * 1024),
    )(
        wins,
        norm_gain.reshape(1, width),
        norm_bias.reshape(1, width),
        qkv_weight.T,
        qkv_weight,
        qkv_bias.reshape(3 * width, 1),
        proj_weight,
    )


def sum_kernel(
    chips, scale, g_ref, out_ref, first_ref, got_ref, mine_ref, parts_ref,
    pair_send, pair_recv, send2, recv2, send3, recv3,
):
    half = g_ref.shape[0] // 2
    chunk = half // chips
    count_z = lax.axis_size("gz")
    core = lax.axis_index("gy")
    me = lax.axis_index("gx") * count_z + lax.axis_index("gz")
    pair = {"gy": 1 - core}

    def chip(step):
        other = lax.rem(me + step, chips)
        return other, {"gx": other // count_z, "gz": lax.rem(other, count_z)}

    barrier = pltpu.get_barrier_semaphore()
    pl.semaphore_signal(barrier, inc=1, device_id=pair, device_id_type=MESH)

    def greet(step, carry):
        pl.semaphore_signal(barrier, inc=1, device_id=chip(step)[1], device_id_type=MESH)
        return carry

    lax.fori_loop(1, chips, greet, 0)
    pl.semaphore_wait(barrier, chips)

    def rows(start, size):
        return pl.ds(pl.multiple_of(start, 16), size)

    first_ref[...] = (g_ref[rows((1 - core) * half, half), :] * scale).astype(jnp.bfloat16)
    copy = pltpu.make_async_remote_copy(
        src_ref=first_ref, dst_ref=got_ref, send_sem=pair_send.at[0], recv_sem=pair_recv.at[0],
        device_id=pair, device_id_type=MESH,
    )
    copy.start()
    copy.wait()
    mine_ref[...] = (
        g_ref[rows(core * half, half), :] * scale + got_ref[...].astype(jnp.float32)
    ).astype(jnp.bfloat16)

    def scatter(step):
        other, device = chip(step)
        return pltpu.make_async_remote_copy(
            src_ref=mine_ref.at[rows(other * chunk, chunk), :],
            dst_ref=parts_ref.at[step],
            send_sem=send2.at[step], recv_sem=recv2.at[step],
            device_id=device, device_id_type=MESH,
        )

    def start_scatter(step, carry):
        scatter(step).start()
        return carry

    def wait_scatter(step, carry):
        scatter(step).wait()
        return carry

    lax.fori_loop(1, chips, start_scatter, 0)
    lax.fori_loop(1, chips, wait_scatter, 0)
    parts_ref[0] = mine_ref[rows(me * chunk, chunk), :]
    place = rows(core * half + me * chunk, chunk)

    def add(step, total):
        return total + parts_ref[step].astype(jnp.float32)

    total = lax.fori_loop(0, chips, add, jnp.zeros((chunk, LANES), jnp.float32))
    out_ref[place, :] = total.astype(jnp.bfloat16)

    def gather(step):
        return pltpu.make_async_remote_copy(
            src_ref=out_ref.at[place, :],
            dst_ref=out_ref.at[place, :],
            send_sem=send3.at[step], recv_sem=recv3.at[step],
            device_id=chip(step)[1], device_id_type=MESH,
        )

    def start_gather(step, carry):
        gather(step).start()
        return carry

    def wait_gather(step, carry):
        gather(step).wait()
        return carry

    lax.fori_loop(1, chips, start_gather, 0)
    lax.fori_loop(1, chips, wait_gather, 0)
    final = rows(core * half, half)
    copy = pltpu.make_async_remote_copy(
        src_ref=out_ref.at[final, :], dst_ref=out_ref.at[final, :],
        send_sem=pair_send.at[1], recv_sem=pair_recv.at[1],
        device_id=pair, device_id_type=MESH,
    )
    copy.start()
    copy.wait()


def summed(grads, chips, scale):
    rows = grads.shape[0]
    half = rows // 2
    return pl.pallas_call(
        functools.partial(sum_kernel, chips, scale),
        out_shape=jax.ShapeDtypeStruct((rows, LANES), jnp.bfloat16),
        in_specs=[pl.BlockSpec(memory_space=pltpu.VMEM)],
        out_specs=pl.BlockSpec(memory_space=pltpu.VMEM),
        scratch_shapes=[
            pltpu.VMEM((half, LANES), jnp.bfloat16),
            pltpu.VMEM((half, LANES), jnp.bfloat16),
            pltpu.VMEM((half, LANES), jnp.bfloat16),
            pltpu.VMEM((chips, half // chips, LANES), jnp.bfloat16),
            pltpu.SemaphoreType.DMA((2,)),
            pltpu.SemaphoreType.DMA((2,)),
            pltpu.SemaphoreType.DMA((chips,)),
            pltpu.SemaphoreType.DMA((chips,)),
            pltpu.SemaphoreType.DMA((chips,)),
            pltpu.SemaphoreType.DMA((chips,)),
        ],
        compiler_params=pltpu.CompilerParams(
            collective_id=1, has_side_effects=True, vmem_limit_bytes=16 * 1024 * 1024
        ),
    )(grads)


def to_cells(block):
    x, y, z, width = block.shape
    shaped = block.reshape(x // SHIFT, SHIFT, y // SHIFT, SHIFT, z // SHIFT, SHIFT, width)
    return shaped.transpose(0, 2, 4, 1, 3, 5, 6).reshape(
        x // SHIFT, y // SHIFT, z // SHIFT, CELL, width
    )


def from_windows(wins, x, y, z):
    width = wins.shape[-1]
    shaped = wins.reshape(
        x // WIN, y // WIN, z // WIN, 2, 2, 2, SHIFT, SHIFT, SHIFT, width
    )
    return shaped.transpose(0, 3, 6, 1, 4, 7, 2, 5, 8, 9).reshape(x, y, z, width)


def per_device(tokens, upstream, norm_gain, norm_bias, qkv_weight, qkv_bias, proj_weight):
    x, y, z, width = tokens.shape
    chips = lax.axis_size("gx") * lax.axis_size("gz")
    devices = chips * lax.axis_size("gy")
    spread = (x // WIN, y // WIN, z // WIN)
    cells = jnp.concatenate([to_cells(tokens), to_cells(upstream)], axis=-1)
    wins = halo(cells)
    step = 16 * devices
    rows = -(-8 * width // step) * step
    out, grads = windows(
        wins, spread, rows, norm_gain, norm_bias, qkv_weight, qkv_bias, proj_weight
    )
    scale = float(x * y * z * devices) ** (-0.5)
    total = summed(grads, chips, scale).astype(jnp.float32)
    rest = width - LANES
    low = total[: 4 * width]
    high = total[4 * width : 8 * width]
    matrix = jnp.concatenate([low, high[:, :rest]], axis=1)
    return (
        from_windows(out, x, y, z),
        matrix[: 3 * width].T,
        high[: 3 * width, rest],
        matrix[3 * width :],
        high[3 * width :, rest],
        high[3 * width :, rest + 1],
        high[3 * width :, rest + 2],
    )


def solution(mesh):
    placed = (P("gx", "gy", "gz", None), P("gx", "gy", "gz", None), P(), P(), P(), P(), P())
    return jax.shard_map(
        per_device,
        mesh=mesh,
        in_specs=placed,
        out_specs=(P("gx", "gy", "gz", None), P(), P(), P(), P(), P(), P()),
        check_vma=False,
    )
```

```python
import functools

import jax
import jax.numpy as jnp
from jax import lax
from jax.experimental import pallas as pl
from jax.experimental.pallas import tpu as pltpu
from jax.sharding import PartitionSpec as P

HEADS = 6
WIN = 8
SHIFT = 4
CELL = SHIFT**3
LANES = 128
MASKED = -1e30
MESH = pl.DeviceIdType.MESH


def dot(left, right):
    return jnp.dot(left, right, preferred_element_type=jnp.float32)


def dot_nt(left, right):
    return lax.dot_general(
        left, right, (((1,), (1,)), ((), ())), preferred_element_type=jnp.float32
    )


def wrapped(value, size):
    return lax.rem(value + size, size)


def rows_at(start, size):
    return pl.ds(pl.multiple_of(start, 16), size)


def cell_order(cells_y, cells_z):
    area = SHIFT * SHIFT
    count = cells_y * cells_z * area
    row = lax.broadcasted_iota(jnp.int32, (count, count), 0)
    column = lax.broadcasted_iota(jnp.int32, (count, count), 1)
    cell, inside = row // area, row % area
    y = cell // cells_z * SHIFT + inside // SHIFT
    z = cell % cells_z * SHIFT + inside % SHIFT
    return jnp.where(column == y * (cells_z * SHIFT) + z, 1.0, 0.0).astype(jnp.bfloat16)


def kernel(
    counts, width, scale, tok_ref, upw_ref, gain_ref, nbias_ref, wt_ref, w_ref, qbias_ref, pw_ref,
    out_ref, qgrad_ref, qbgrad_ref, pgrad_ref, small_ref,
    cells_ref, wins_ref, res_ref, hid_ref, normed_ref, inv_ref, pk_ref, da_ref, att_ref, pg_ref,
    accq_ref, accp_ref, accs_ref, g_ref, tot_ref, first_ref, got_ref, mine_ref, parts_ref,
    send_sem, recv_sem, local_sem, pair_send, pair_recv, send2, recv2, send3, recv3,
):
    axes = ("gx", "gy", "gz")
    here = [lax.axis_index(axis) for axis in axes]
    sizes = [lax.axis_size(axis) for axis in axes]
    devices = sizes[0] * sizes[1] * sizes[2]
    chips = sizes[0] * sizes[2]
    core = here[1]
    me = here[0] * sizes[2] + here[2]
    spread = [count // 2 for count in counts]
    cells = counts[0] * counts[1] * counts[2]
    length = WIN**3
    area = SHIFT * SHIFT
    plane = counts[1] * counts[2] * area
    head = width // HEADS
    factor = head ** (-0.5)
    single = jnp.float32
    half = jnp.bfloat16

    barrier = pltpu.get_barrier_semaphore()
    rank = (here[0] * sizes[1] + here[1]) * sizes[2] + here[2]

    def greet(step, carry):
        other = lax.rem(rank + step, devices)
        place = {
            "gx": other // (sizes[1] * sizes[2]),
            "gy": lax.rem(other // sizes[2], sizes[1]),
            "gz": lax.rem(other, sizes[2]),
        }
        pl.semaphore_signal(barrier, inc=1, device_id=place, device_id_type=MESH)
        return carry

    lax.fori_loop(1, devices, greet, 0)

    order = cell_order(counts[1], counts[2])
    for x in range(counts[0] * SHIFT):
        inside = slice(x % SHIFT * area, (x % SHIFT + 1) * area)
        for source, lanes in ((tok_ref, slice(0, width)), (upw_ref, slice(width, 2 * width))):
            moved = dot(order, source[x].reshape(plane, width)).astype(half)
            cells_ref[x // SHIFT, :, inside, lanes] = moved.reshape(-1, area, width)
    pl.semaphore_wait(barrier, devices - 1)

    arriving = {}
    for a in range(counts[0]):
        for b in range(counts[1]):
            for c in range(counts[2]):
                offset = tuple(int(at == 0) for at in (a, b, c))
                to = [(at - 1) % count for at, count in zip((a, b, c), counts)]
                window = (to[0] // 2 * spread[1] + to[1] // 2) * spread[2] + to[2] // 2
                octant = (to[0] % 2 * 2 + to[1] % 2) * 2 + to[2] % 2
                number = window * 8 + octant
                source = cells_ref.at[a, b * counts[2] + c]
                target = wins_ref.at[window, octant]
                if any(offset):
                    copy = pltpu.make_async_remote_copy(
                        src_ref=source,
                        dst_ref=target,
                        send_sem=send_sem.at[number],
                        recv_sem=recv_sem.at[number],
                        device_id={
                            axis: wrapped(at - step, size)
                            for axis, at, step, size in zip(axes, here, offset, sizes)
                        },
                        device_id_type=MESH,
                    )
                else:
                    copy = pltpu.make_async_copy(source, target, local_sem.at[number])
                arriving[number] = (copy, any(offset))
    for number in sorted(arriving):
        arriving[number][0].start()

    hid_ref[...] = jnp.ones_like(hid_ref)
    accq_ref[...] = jnp.zeros_like(accq_ref)
    accp_ref[...] = jnp.zeros_like(accp_ref)
    accs_ref[...] = jnp.zeros_like(accs_ref)
    tile = min(256, length)
    exponent = factor * 1.4426950408889634

    def one_window(step, nothing):
        for window in range(cells // 8):

            @pl.when(step == window)
            def _():
                for octant in range(8):
                    copy, remote = arriving[window * 8 + octant]
                    if remote:
                        copy.wait_recv()
                    else:
                        copy.wait()

        both = wins_ref[step].reshape(length, 2 * width)
        inputs = both[:, :width].astype(single)
        up = both[:, width:]
        centred = inputs - jnp.mean(inputs, axis=-1, keepdims=True)
        inverse = lax.rsqrt(jnp.mean(centred * centred, axis=-1, keepdims=True) + 1e-05)
        normed = centred * inverse
        normed_ref[...] = normed
        inv_ref[...] = inverse
        hidden = (normed * gain_ref[...] + nbias_ref[...]).astype(half)
        hid_ref[:, :width] = hidden
        pk_ref[...] = (dot_nt(wt_ref[...], hidden) + qbias_ref[...]).astype(half)
        da_ref[...] = dot_nt(pw_ref[...], up).astype(half)

        place = (step // (spread[1] * spread[2]), step // spread[2] % spread[1], step % spread[2])
        cut = [
            jnp.where((at == size - 1) & (mine == count - 1), 1, 0)
            for at, size, mine, count in zip(here, sizes, place, spread)
        ]
        octants = lax.broadcasted_iota(jnp.int32, (16, length), 1) // CELL
        region = octants & (cut[0] * 4 + cut[1] * 2 + cut[2])
        own = region == lax.broadcasted_iota(jnp.int32, (16, length), 0)
        mark_q = jnp.where(own, 1.0, 0.0).astype(half)
        mark_k = jnp.where(own, 0.0, MASKED).astype(half)

        def one_head(h, carry):
            base = pl.multiple_of(h * head, head)
            qt = pk_ref[pl.ds(base, head), :]
            kt = pk_ref[pl.ds(base + width, head), :]
            vt = pk_ref[pl.ds(base + 2 * width, head), :]
            dat = da_ref[pl.ds(base, head), :]
            qt_marked = jnp.concatenate([qt, mark_q], axis=0)
            keys = jnp.concatenate([kt, mark_k], axis=0).T
            values = vt.T
            kg = jnp.zeros((head, length), single)
            vg = jnp.zeros((head, length), single)
            for start in range(0, length, tile):
                part = slice(start, start + tile)
                scores = dot(keys, qt_marked[:, part])
                prob_grad = dot(values, dat[:, part])
                peak = jnp.max(scores, axis=0, keepdims=True)
                expo = jnp.exp2((scores - peak) * exponent)
                probs = expo * (1.0 / jnp.sum(expo, axis=0, keepdims=True))
                inner = jnp.sum(probs * prob_grad, axis=0, keepdims=True)
                probs_half = probs.astype(half)
                score_grad = (probs * (prob_grad - inner)).astype(half)
                att_ref[pl.ds(base, head), part] = dot(vt, probs_half).astype(half)
                pg_ref[pl.ds(base, head), part] = (dot(kt, score_grad) * factor).astype(half)
                vg += dot_nt(dat[:, part], probs_half)
                kg += dot_nt(qt[:, part], score_grad)
            pg_ref[pl.ds(base + width, head), :] = (kg * factor).astype(half)
            pg_ref[pl.ds(base + 2 * width, head), :] = vg.astype(half)
            return carry

        lax.fori_loop(0, HEADS, one_head, 0, unroll=1)

        accq_ref[...] += dot(pg_ref[...], hid_ref[...])
        accp_ref[...] += dot(att_ref[...], up)
        hidden_grad = dot(w_ref[...], pg_ref[...]).T
        normed = normed_ref[...]
        up_single = up.astype(single)
        accs_ref[0:1, :] += jnp.sum(up_single, axis=0, keepdims=True)
        accs_ref[1:2, :] += jnp.sum(hidden_grad * normed, axis=0, keepdims=True)
        accs_ref[2:3, :] += jnp.sum(hidden_grad, axis=0, keepdims=True)
        normed_grad = hidden_grad * gain_ref[...]
        first = jnp.mean(normed_grad, axis=-1, keepdims=True)
        second = jnp.mean(normed_grad * normed, axis=-1, keepdims=True)
        token_grad = up_single + inv_ref[...] * (normed_grad - first - normed * second)
        res_ref[step] = token_grad.astype(half).reshape(8, CELL, width)
        return nothing

    lax.fori_loop(0, cells // 8, one_window, 0)

    total_rows = g_ref.shape[0]
    rest = width - LANES
    low = 4 * width
    last = slice(low + 3 * width, 2 * low)
    if total_rows > 2 * low:
        g_ref[2 * low :, :] = jnp.zeros((total_rows - 2 * low, LANES), single)
    g_ref[: 3 * width, :] = accq_ref[:, :LANES]
    g_ref[3 * width : low, :] = accp_ref[:, :LANES]
    g_ref[low : low + 3 * width, :] = accq_ref[:, LANES:]
    g_ref[last, :] = jnp.zeros((width, LANES), single)
    g_ref[last, :rest] = accp_ref[:, LANES:]
    g_ref[last, rest : rest + 8] = accs_ref[...].T

    middle = total_rows // 2
    chunk = middle // chips
    pair = {"gy": 1 - core}

    def chip(step):
        other = lax.rem(me + step, chips)
        return other, {"gx": other // sizes[2], "gz": lax.rem(other, sizes[2])}

    first_ref[...] = (g_ref[rows_at((1 - core) * middle, middle), :] * scale).astype(half)
    swap = pltpu.make_async_remote_copy(
        src_ref=first_ref, dst_ref=got_ref, send_sem=pair_send.at[0], recv_sem=pair_recv.at[0],
        device_id=pair, device_id_type=MESH,
    )
    swap.start()
    for number in sorted(arriving):
        if arriving[number][1]:
            arriving[number][0].wait_send()
    swap.wait()
    mine_ref[...] = (
        g_ref[rows_at(core * middle, middle), :] * scale + got_ref[...].astype(single)
    ).astype(half)

    def scatter(step):
        other, device = chip(step)
        return pltpu.make_async_remote_copy(
            src_ref=mine_ref.at[rows_at(other * chunk, chunk), :],
            dst_ref=parts_ref.at[step],
            send_sem=send2.at[step], recv_sem=recv2.at[step],
            device_id=device, device_id_type=MESH,
        )

    def start_scatter(step, carry):
        scatter(step).start()
        return carry

    def wait_scatter(step, carry):
        scatter(step).wait()
        return carry

    lax.fori_loop(1, chips, start_scatter, 0)

    def put_back(first_x, last_x):
        for x in range(first_x, last_x):
            inside = slice(x % SHIFT * area, (x % SHIFT + 1) * area)
            pieces = []
            for b in range(counts[1]):
                for c in range(counts[2]):
                    a = x // SHIFT
                    window = (a // 2 * spread[1] + b // 2) * spread[2] + c // 2
                    octant = (a % 2 * 2 + b % 2) * 2 + c % 2
                    pieces.append(res_ref[window, octant, inside, :])
            moved = lax.dot_general(
                order, jnp.concatenate(pieces, axis=0), (((0,), (0,)), ((), ())),
                preferred_element_type=single,
            )
            out_ref[x] = moved.astype(half).reshape(out_ref.shape[1:])

    planes = counts[0] * SHIFT
    put_back(0, planes // 2)
    lax.fori_loop(1, chips, wait_scatter, 0)
    parts_ref[0] = mine_ref[rows_at(me * chunk, chunk), :]
    spot = rows_at(core * middle + me * chunk, chunk)

    def add(step, total):
        return total + parts_ref[step].astype(single)

    total = lax.fori_loop(0, chips, add, jnp.zeros((chunk, LANES), single))
    tot_ref[spot, :] = total.astype(half)

    def gather(step):
        return pltpu.make_async_remote_copy(
            src_ref=tot_ref.at[spot, :],
            dst_ref=tot_ref.at[spot, :],
            send_sem=send3.at[step], recv_sem=recv3.at[step],
            device_id=chip(step)[1], device_id_type=MESH,
        )

    def start_gather(step, carry):
        gather(step).start()
        return carry

    def wait_gather(step, carry):
        gather(step).wait()
        return carry

    lax.fori_loop(1, chips, start_gather, 0)
    put_back(planes // 2, planes)
    lax.fori_loop(1, chips, wait_gather, 0)
    final = rows_at(core * middle, middle)
    swap = pltpu.make_async_remote_copy(
        src_ref=tot_ref.at[final, :], dst_ref=tot_ref.at[final, :],
        send_sem=pair_send.at[1], recv_sem=pair_recv.at[1],
        device_id=pair, device_id_type=MESH,
    )
    swap.start()
    swap.wait()
    qgrad_ref[:LANES, :] = tot_ref[: 3 * width, :].astype(single).T
    high = tot_ref[low : low + 3 * width, :].astype(single).T
    qgrad_ref[LANES:, :] = high[:rest]
    qbgrad_ref[...] = high[rest : rest + 1]
    ends = tot_ref[last, :].astype(single)
    pgrad_ref[:, :LANES] = tot_ref[3 * width : low, :].astype(single)
    pgrad_ref[:, LANES:] = ends[:, :rest]
    small_ref[...] = ends.T[rest : rest + 8]


def per_device(tokens, upstream, norm_gain, norm_bias, qkv_weight, qkv_bias, proj_weight):
    x, y, z, width = tokens.shape
    chips = lax.axis_size("gx") * lax.axis_size("gz")
    devices = chips * lax.axis_size("gy")
    counts = (x // SHIFT, y // SHIFT, z // SHIFT)
    cells = counts[0] * counts[1] * counts[2]
    length = WIN**3
    step = 16 * devices
    rows = -(-8 * width // step) * step
    middle = rows // 2
    scale = float(x * y * z * devices) ** (-0.5)
    vmem = pl.BlockSpec(memory_space=pltpu.VMEM)
    half = jnp.bfloat16
    single = jnp.float32
    dma = pltpu.SemaphoreType.DMA
    token_grad, qgrad, qbgrad, pgrad, small = pl.pallas_call(
        functools.partial(kernel, counts, width, scale),
        out_shape=(
            jax.ShapeDtypeStruct(tokens.shape, half),
            jax.ShapeDtypeStruct((width, 3 * width), single),
            jax.ShapeDtypeStruct((1, 3 * width), single),
            jax.ShapeDtypeStruct((width, width), single),
            jax.ShapeDtypeStruct((8, width), single),
        ),
        in_specs=[vmem] * 8,
        out_specs=(vmem,) * 5,
        scratch_shapes=[
            pltpu.VMEM((counts[0], counts[1] * counts[2], CELL, 2 * width), half),
            pltpu.VMEM((cells // 8, 8, CELL, 2 * width), half),
            pltpu.VMEM((cells // 8, 8, CELL, width), half),
            pltpu.VMEM((length, 2 * LANES), half),
            pltpu.VMEM((length, width), single),
            pltpu.VMEM((length, 1), single),
            pltpu.VMEM((3 * width, length), half),
            pltpu.VMEM((width, length), half),
            pltpu.VMEM((width, length), half),
            pltpu.VMEM((3 * width, length), half),
            pltpu.VMEM((3 * width, 2 * LANES), single),
            pltpu.VMEM((width, width), single),
            pltpu.VMEM((8, width), single),
            pltpu.VMEM((rows, LANES), single),
            pltpu.VMEM((rows, LANES), half),
            pltpu.VMEM((middle, LANES), half),
            pltpu.VMEM((middle, LANES), half),
            pltpu.VMEM((middle, LANES), half),
            pltpu.VMEM((chips, middle // chips, LANES), half),
            dma((cells,)),
            dma((cells,)),
            dma((cells,)),
            dma((2,)),
            dma((2,)),
            dma((chips,)),
            dma((chips,)),
            dma((chips,)),
            dma((chips,)),
        ],
        compiler_params=pltpu.CompilerParams(
            collective_id=0, has_side_effects=True, vmem_limit_bytes=48 * 1024 * 1024
        ),
    )(
        tokens,
        upstream,
        norm_gain.reshape(1, width),
        norm_bias.reshape(1, width),
        qkv_weight.T,
        qkv_weight,
        qkv_bias.reshape(3 * width, 1),
        proj_weight,
    )
    return (token_grad, qgrad, qbgrad[0], pgrad, small[0], small[1], small[2])


def solution(mesh):
    placed = (P("gx", "gy", "gz", None), P("gx", "gy", "gz", None), P(), P(), P(), P(), P())
    return jax.shard_map(
        per_device,
        mesh=mesh,
        in_specs=placed,
        out_specs=(P("gx", "gy", "gz", None), P(), P(), P(), P(), P(), P()),
        check_vma=False,
    )
```

```python
import functools

import jax
import jax.numpy as jnp
from jax import lax
from jax.experimental import pallas as pl
from jax.experimental.pallas import tpu as pltpu
from jax.sharding import PartitionSpec as P

HEADS = 6
WIN = 8
SHIFT = 4
CELL = SHIFT**3
LANES = 128
MASKED = -1e30
MESH = pl.DeviceIdType.MESH


def dot(left, right):
    return jnp.dot(left, right, preferred_element_type=jnp.float32)


def dot_nt(left, right):
    return lax.dot_general(
        left, right, (((1,), (1,)), ((), ())), preferred_element_type=jnp.float32
    )


def wrapped(value, size):
    return lax.rem(value + size, size)


def rows_at(start, size):
    return pl.ds(pl.multiple_of(start, 16), size)


def cell_order(cells_y, cells_z):
    area = SHIFT * SHIFT
    count = cells_y * cells_z * area
    row = lax.broadcasted_iota(jnp.int32, (count, count), 0)
    column = lax.broadcasted_iota(jnp.int32, (count, count), 1)
    cell, inside = row // area, row % area
    y = cell // cells_z * SHIFT + inside // SHIFT
    z = cell % cells_z * SHIFT + inside % SHIFT
    return jnp.where(column == y * (cells_z * SHIFT) + z, 1.0, 0.0).astype(jnp.bfloat16)


def kernel(
    counts, width, scale, tok_hbm, upw_hbm, gain_ref, nbias_ref, w_ref, qbias_ref, pw_ref,
    out_ref, qgrad_ref, qbgrad_ref, pgrad_ref, small_ref,
    tok_ref, upw_ref, wt_ref, cells_ref, wins_ref, res_ref, hid_ref, normed_ref, inv_ref, pk_ref, da_ref, att_ref, pg_ref,
    accq_ref, accp_ref, accs_ref, g_ref, tot_ref, first_ref, got_ref, mine_ref, parts_ref,
    load_sem, send_sem, recv_sem, local_sem, pair_send, pair_recv, send2, recv2, send3, recv3,
):
    axes = ("gx", "gy", "gz")
    here = [lax.axis_index(axis) for axis in axes]
    sizes = [lax.axis_size(axis) for axis in axes]
    devices = sizes[0] * sizes[1] * sizes[2]
    chips = sizes[0] * sizes[2]
    core = here[1]
    me = here[0] * sizes[2] + here[2]
    spread = [count // 2 for count in counts]
    cells = counts[0] * counts[1] * counts[2]
    length = WIN**3
    area = SHIFT * SHIFT
    plane = counts[1] * counts[2] * area
    head = width // HEADS
    factor = head ** (-0.5)
    single = jnp.float32
    half = jnp.bfloat16

    loads = []
    for a in range(counts[0]):
        planes = pl.ds(a * SHIFT, SHIFT)
        for n, (source, target) in enumerate(((tok_hbm, tok_ref), (upw_hbm, upw_ref))):
            loads.append(
                pltpu.make_async_copy(
                    source.at[planes], target.at[planes], load_sem.at[2 * a + n]
                )
            )
    for load in loads:
        load.start()

    barrier = pltpu.get_barrier_semaphore()
    rank = (here[0] * sizes[1] + here[1]) * sizes[2] + here[2]

    def greet(step, carry):
        other = lax.rem(rank + step, devices)
        place = {
            "gx": other // (sizes[1] * sizes[2]),
            "gy": lax.rem(other // sizes[2], sizes[1]),
            "gz": lax.rem(other, sizes[2]),
        }
        pl.semaphore_signal(barrier, inc=1, device_id=place, device_id_type=MESH)
        return carry

    lax.fori_loop(1, devices, greet, 0)

    order = cell_order(counts[1], counts[2])

    def take_in(a):
        for source, load, start in ((tok_ref, loads[2 * a], 0), (upw_ref, loads[2 * a + 1], width)):
            load.wait()
            for x in range(SHIFT):
                moved = dot(order, source[a * SHIFT + x].reshape(plane, width)).astype(half)
                cells_ref[a, :, x * area : (x + 1) * area, start : start + width] = moved.reshape(
                    -1, area, width
                )

    arriving = {}
    for a in range(counts[0]):
        for b in range(counts[1]):
            for c in range(counts[2]):
                offset = tuple(int(at == 0) for at in (a, b, c))
                to = [(at - 1) % count for at, count in zip((a, b, c), counts)]
                window = (to[0] // 2 * spread[1] + to[1] // 2) * spread[2] + to[2] // 2
                octant = (to[0] % 2 * 2 + to[1] % 2) * 2 + to[2] % 2
                number = window * 8 + octant
                source = cells_ref.at[a, b * counts[2] + c]
                target = wins_ref.at[window, octant]
                if any(offset):
                    copy = pltpu.make_async_remote_copy(
                        src_ref=source,
                        dst_ref=target,
                        send_sem=send_sem.at[number],
                        recv_sem=recv_sem.at[number],
                        device_id={
                            axis: wrapped(at - step, size)
                            for axis, at, step, size in zip(axes, here, offset, sizes)
                        },
                        device_id_type=MESH,
                    )
                else:
                    copy = pltpu.make_async_copy(source, target, local_sem.at[number])
                arriving[number] = (copy, any(offset))

    def send(window, remote):
        for octant in range(8):
            copy, far = arriving[window * 8 + octant]
            if far == remote:
                copy.start()

    take_in(0)
    pl.semaphore_wait(barrier, devices - 1)
    early = counts[0] == 2 and min(counts[1:]) > 2
    if early:
        send(0, True)
    for a in range(1, counts[0]):
        take_in(a)
    if not early:
        send(0, True)
    send(0, False)
    wt_ref[...] = w_ref[...].T
    hid_ref[...] = jnp.ones_like(hid_ref)
    accq_ref[...] = jnp.zeros_like(accq_ref)
    accp_ref[...] = jnp.zeros_like(accp_ref)
    accs_ref[...] = jnp.zeros_like(accs_ref)
    tile = min(256, length)
    exponent = factor * 1.4426950408889634

    def one_window(step, nothing):
        for window in range(cells // 8):

            @pl.when(step == window)
            def _():
                for octant in range(8):
                    copy, remote = arriving[window * 8 + octant]
                    if remote:
                        copy.wait_recv()
                    else:
                        copy.wait()
                for later in {0: (1, 2)}.get(window, (window + 2,)):
                    if later < cells // 8:
                        send(later, True)
                        send(later, False)

        both = wins_ref[step].reshape(length, 2 * width)
        inputs = both[:, :width].astype(single)
        up = both[:, width:]
        centred = inputs - jnp.mean(inputs, axis=-1, keepdims=True)
        inverse = lax.rsqrt(jnp.mean(centred * centred, axis=-1, keepdims=True) + 1e-05)
        normed = centred * inverse
        normed_ref[...] = normed
        inv_ref[...] = inverse
        hidden = (normed * gain_ref[...] + nbias_ref[...]).astype(half)
        hid_ref[:, :width] = hidden
        pk_ref[...] = (dot_nt(wt_ref[...], hidden) + qbias_ref[...]).astype(half)
        da_ref[...] = dot_nt(pw_ref[...], up).astype(half)

        place = (step // (spread[1] * spread[2]), step // spread[2] % spread[1], step % spread[2])
        cut = [
            jnp.where((at == size - 1) & (mine == count - 1), 1, 0)
            for at, size, mine, count in zip(here, sizes, place, spread)
        ]
        octants = lax.broadcasted_iota(jnp.int32, (16, length), 1) // CELL
        region = octants & (cut[0] * 4 + cut[1] * 2 + cut[2])
        own = region == lax.broadcasted_iota(jnp.int32, (16, length), 0)
        mark_q = jnp.where(own, 1.0, 0.0).astype(half)
        mark_k = jnp.where(own, 0.0, MASKED).astype(half)

        def one_head(h, carry):
            base = pl.multiple_of(h * head, head)
            qt = pk_ref[pl.ds(base, head), :]
            kt = pk_ref[pl.ds(base + width, head), :]
            vt = pk_ref[pl.ds(base + 2 * width, head), :]
            dat = da_ref[pl.ds(base, head), :]
            qt_marked = jnp.concatenate([qt, mark_q], axis=0)
            keys = jnp.concatenate([kt, mark_k], axis=0).T
            values = vt.T
            kg = jnp.zeros((head, length), single)
            vg = jnp.zeros((head, length), single)
            for start in range(0, length, tile):
                part = slice(start, start + tile)
                scores = dot(keys, qt_marked[:, part])
                prob_grad = dot(values, dat[:, part])
                peak = jnp.max(scores, axis=0, keepdims=True)
                expo = jnp.exp2((scores - peak) * exponent)
                probs = expo * (1.0 / jnp.sum(expo, axis=0, keepdims=True))
                inner = jnp.sum(probs * prob_grad, axis=0, keepdims=True)
                probs_half = probs.astype(half)
                score_grad = (probs * (prob_grad - inner)).astype(half)
                att_ref[pl.ds(base, head), part] = dot(vt, probs_half).astype(half)
                pg_ref[pl.ds(base, head), part] = (dot(kt, score_grad) * factor).astype(half)
                vg += dot_nt(dat[:, part], probs_half)
                kg += dot_nt(qt[:, part], score_grad)
            pg_ref[pl.ds(base + width, head), :] = (kg * factor).astype(half)
            pg_ref[pl.ds(base + 2 * width, head), :] = vg.astype(half)
            return carry

        lax.fori_loop(0, HEADS, one_head, 0, unroll=6)

        accq_ref[...] += dot(pg_ref[...], hid_ref[...])
        accp_ref[...] += dot(att_ref[...], up)
        hidden_grad = dot(w_ref[...], pg_ref[...]).T
        normed = normed_ref[...]
        up_single = up.astype(single)
        accs_ref[0:1, :] += jnp.sum(up_single, axis=0, keepdims=True)
        accs_ref[1:2, :] += jnp.sum(hidden_grad * normed, axis=0, keepdims=True)
        accs_ref[2:3, :] += jnp.sum(hidden_grad, axis=0, keepdims=True)
        normed_grad = hidden_grad * gain_ref[...]
        first = jnp.mean(normed_grad, axis=-1, keepdims=True)
        second = jnp.mean(normed_grad * normed, axis=-1, keepdims=True)
        token_grad = up_single + inv_ref[...] * (normed_grad - first - normed * second)
        res_ref[step] = token_grad.astype(half).reshape(8, CELL, width)
        return nothing

    lax.fori_loop(0, cells // 8, one_window, 0)

    total_rows = g_ref.shape[0]
    rest = width - LANES
    low = 4 * width
    last = slice(low + 3 * width, 2 * low)
    if total_rows > 2 * low:
        g_ref[2 * low :, :] = jnp.zeros((total_rows - 2 * low, LANES), single)
    g_ref[: 3 * width, :] = accq_ref[:, :LANES]
    g_ref[3 * width : low, :] = accp_ref[:, :LANES]
    g_ref[low : low + 3 * width, :] = accq_ref[:, LANES:]
    g_ref[last, :] = jnp.zeros((width, LANES), single)
    g_ref[last, :rest] = accp_ref[:, LANES:]
    g_ref[last, rest : rest + 8] = accs_ref[...].T

    middle = total_rows // 2
    chunk = middle // chips
    pair = {"gy": 1 - core}

    def chip(step):
        other = lax.rem(me + step, chips)
        return other, {"gx": other // sizes[2], "gz": lax.rem(other, sizes[2])}

    first_ref[...] = (g_ref[rows_at((1 - core) * middle, middle), :] * scale).astype(half)
    swap = pltpu.make_async_remote_copy(
        src_ref=first_ref, dst_ref=got_ref, send_sem=pair_send.at[0], recv_sem=pair_recv.at[0],
        device_id=pair, device_id_type=MESH,
    )
    swap.start()
    for number in sorted(arriving):
        if arriving[number][1]:
            arriving[number][0].wait_send()
    swap.wait()
    mine_ref[...] = (
        g_ref[rows_at(core * middle, middle), :] * scale + got_ref[...].astype(single)
    ).astype(half)

    def scatter(step):
        other, device = chip(step)
        return pltpu.make_async_remote_copy(
            src_ref=mine_ref.at[rows_at(other * chunk, chunk), :],
            dst_ref=parts_ref.at[step],
            send_sem=send2.at[step], recv_sem=recv2.at[step],
            device_id=device, device_id_type=MESH,
        )

    def start_scatter(step, carry):
        scatter(step).start()
        return carry

    def wait_scatter(step, carry):
        scatter(step).wait()
        return carry

    lax.fori_loop(1, chips, start_scatter, 0)

    def put_back(first_x, last_x):
        for x in range(first_x, last_x):
            inside = slice(x % SHIFT * area, (x % SHIFT + 1) * area)
            pieces = []
            for b in range(counts[1]):
                for c in range(counts[2]):
                    a = x // SHIFT
                    window = (a // 2 * spread[1] + b // 2) * spread[2] + c // 2
                    octant = (a % 2 * 2 + b % 2) * 2 + c % 2
                    pieces.append(res_ref[window, octant, inside, :])
            moved = lax.dot_general(
                order, jnp.concatenate(pieces, axis=0), (((0,), (0,)), ((), ())),
                preferred_element_type=single,
            )
            out_ref[x] = moved.astype(half).reshape(out_ref.shape[1:])

    planes = counts[0] * SHIFT
    put_back(0, planes // 2)
    lax.fori_loop(1, chips, wait_scatter, 0)
    parts_ref[0] = mine_ref[rows_at(me * chunk, chunk), :]
    spot = rows_at(core * middle + me * chunk, chunk)

    def add(step, total):
        return total + parts_ref[step].astype(single)

    total = lax.fori_loop(0, chips, add, jnp.zeros((chunk, LANES), single))
    tot_ref[spot, :] = total.astype(half)

    def gather(step):
        return pltpu.make_async_remote_copy(
            src_ref=tot_ref.at[spot, :],
            dst_ref=tot_ref.at[spot, :],
            send_sem=send3.at[step], recv_sem=recv3.at[step],
            device_id=chip(step)[1], device_id_type=MESH,
        )

    def start_gather(step, carry):
        gather(step).start()
        return carry

    def wait_gather(step, carry):
        gather(step).wait()
        return carry

    lax.fori_loop(1, chips, start_gather, 0)
    put_back(planes // 2, planes)
    lax.fori_loop(1, chips, wait_gather, 0)
    final = rows_at(core * middle, middle)
    swap = pltpu.make_async_remote_copy(
        src_ref=tot_ref.at[final, :], dst_ref=tot_ref.at[final, :],
        send_sem=pair_send.at[1], recv_sem=pair_recv.at[1],
        device_id=pair, device_id_type=MESH,
    )
    swap.start()
    swap.wait()
    qgrad_ref[:LANES, :] = tot_ref[: 3 * width, :].astype(single).T
    high = tot_ref[low : low + 3 * width, :].astype(single).T
    qgrad_ref[LANES:, :] = high[:rest]
    qbgrad_ref[...] = high[rest : rest + 1]
    ends = tot_ref[last, :].astype(single)
    pgrad_ref[:, :LANES] = tot_ref[3 * width : low, :].astype(single)
    pgrad_ref[:, LANES:] = ends[:, :rest]
    small_ref[...] = ends.T[rest : rest + 8]


def per_device(tokens, upstream, norm_gain, norm_bias, qkv_weight, qkv_bias, proj_weight):
    x, y, z, width = tokens.shape
    chips = lax.axis_size("gx") * lax.axis_size("gz")
    devices = chips * lax.axis_size("gy")
    counts = (x // SHIFT, y // SHIFT, z // SHIFT)
    cells = counts[0] * counts[1] * counts[2]
    length = WIN**3
    step = 16 * devices
    rows = -(-8 * width // step) * step
    middle = rows // 2
    scale = float(x * y * z * devices) ** (-0.5)
    vmem = pl.BlockSpec(memory_space=pltpu.VMEM)
    half = jnp.bfloat16
    single = jnp.float32
    dma = pltpu.SemaphoreType.DMA
    token_grad, qgrad, qbgrad, pgrad, small = pl.pallas_call(
        functools.partial(kernel, counts, width, scale),
        out_shape=(
            jax.ShapeDtypeStruct(tokens.shape, half),
            jax.ShapeDtypeStruct((width, 3 * width), single),
            jax.ShapeDtypeStruct((1, 3 * width), single),
            jax.ShapeDtypeStruct((width, width), single),
            jax.ShapeDtypeStruct((8, width), single),
        ),
        in_specs=[pl.BlockSpec(memory_space=pl.ANY)] * 2 + [vmem] * 5,
        out_specs=(vmem,) * 5,
        scratch_shapes=[
            pltpu.VMEM(tokens.shape, half),
            pltpu.VMEM(tokens.shape, half),
            pltpu.VMEM((3 * width, width), half),
            pltpu.VMEM((counts[0], counts[1] * counts[2], CELL, 2 * width), half),
            pltpu.VMEM((cells // 8, 8, CELL, 2 * width), half),
            pltpu.VMEM((cells // 8, 8, CELL, width), half),
            pltpu.VMEM((length, 2 * LANES), half),
            pltpu.VMEM((length, width), single),
            pltpu.VMEM((length, 1), single),
            pltpu.VMEM((3 * width, length), half),
            pltpu.VMEM((width, length), half),
            pltpu.VMEM((width, length), half),
            pltpu.VMEM((3 * width, length), half),
            pltpu.VMEM((3 * width, 2 * LANES), single),
            pltpu.VMEM((width, width), single),
            pltpu.VMEM((8, width), single),
            pltpu.VMEM((rows, LANES), single),
            pltpu.VMEM((rows, LANES), half),
            pltpu.VMEM((middle, LANES), half),
            pltpu.VMEM((middle, LANES), half),
            pltpu.VMEM((middle, LANES), half),
            pltpu.VMEM((chips, middle // chips, LANES), half),
            dma((2 * counts[0],)),
            dma((cells,)),
            dma((cells,)),
            dma((cells,)),
            dma((2,)),
            dma((2,)),
            dma((chips,)),
            dma((chips,)),
            dma((chips,)),
            dma((chips,)),
        ],
        compiler_params=pltpu.CompilerParams(
            collective_id=0, has_side_effects=True, vmem_limit_bytes=48 * 1024 * 1024
        ),
    )(
        tokens,
        upstream,
        norm_gain.reshape(1, width),
        norm_bias.reshape(1, width),
        qkv_weight,
        qkv_bias.reshape(3 * width, 1),
        proj_weight,
    )
    return (token_grad, qgrad, qbgrad[0], pgrad, small[0], small[1], small[2])


def solution(mesh):
    placed = (P("gx", "gy", "gz", None), P("gx", "gy", "gz", None), P(), P(), P(), P(), P())
    return jax.shard_map(
        per_device,
        mesh=mesh,
        in_specs=placed,
        out_specs=(P("gx", "gy", "gz", None), P(), P(), P(), P(), P(), P()),
        check_vma=False,
    )
```

```python
import functools

import jax
import jax.numpy as jnp
from jax import lax
from jax.experimental import pallas as pl
from jax.experimental.pallas import tpu as pltpu
from jax.sharding import PartitionSpec as P

HEADS = 6
WIN = 8
SHIFT = 4
CELL = SHIFT**3
LANES = 128
STRIP = 128
MASKED = -1e30
MESH = pl.DeviceIdType.MESH


def dot(left, right):
    return jnp.dot(left, right, preferred_element_type=jnp.float32)


def dot_nt(left, right):
    return lax.dot_general(
        left, right, (((1,), (1,)), ((), ())), preferred_element_type=jnp.float32
    )


def wrapped(value, size):
    return lax.rem(value + size, size)


def rows_at(start, size):
    return pl.ds(pl.multiple_of(start, 16), size)


def cell_order(cells_y, cells_z):
    area = SHIFT * SHIFT
    count = cells_y * cells_z * area
    row = lax.broadcasted_iota(jnp.int32, (count, count), 0)
    column = lax.broadcasted_iota(jnp.int32, (count, count), 1)
    cell, inside = row // area, row % area
    y = cell // cells_z * SHIFT + inside // SHIFT
    z = cell % cells_z * SHIFT + inside % SHIFT
    return jnp.where(column == y * (cells_z * SHIFT) + z, 1.0, 0.0).astype(jnp.bfloat16)


def kernel(
    counts, width, scale, tok_hbm, upw_hbm, gain_ref, nbias_ref, w_hbm, qbias_ref, pw_hbm,
    out_ref, qgrad_ref, qbgrad_ref, pgrad_ref, small_ref,
    tok_ref, upw_ref, w_ref, pw_ref, wt_ref, cells_ref, wins_ref, res_ref, hid_ref, normed_ref, inv_ref, pk_ref, da_ref, att_ref, pg_ref,
    accq_ref, accp_ref, accs_ref, s_ref, d_ref, ph_ref, ds_ref, qb_ref, g_ref, tot_ref, first_ref, got_ref, mine_ref, parts_ref,
    load_sem, send_sem, recv_sem, local_sem, pair_send, pair_recv, send2, recv2, send3, recv3,
):
    axes = ("gx", "gy", "gz")
    here = [lax.axis_index(axis) for axis in axes]
    sizes = [lax.axis_size(axis) for axis in axes]
    devices = sizes[0] * sizes[1] * sizes[2]
    chips = sizes[0] * sizes[2]
    core = here[1]
    me = here[0] * sizes[2] + here[2]
    spread = [count // 2 for count in counts]
    cells = counts[0] * counts[1] * counts[2]
    length = WIN**3
    area = SHIFT * SHIFT
    plane = counts[1] * counts[2] * area
    head = width // HEADS
    factor = head ** (-0.5)
    single = jnp.float32
    half = jnp.bfloat16

    loads = []
    for a in range(counts[0]):
        planes = pl.ds(a * SHIFT, SHIFT)
        for n, (source, target) in enumerate(((tok_hbm, tok_ref), (upw_hbm, upw_ref))):
            loads.append(
                pltpu.make_async_copy(
                    source.at[planes], target.at[planes], load_sem.at[2 * a + n]
                )
            )
    for n, (source, target) in enumerate(((w_hbm, w_ref), (pw_hbm, pw_ref))):
        loads.append(pltpu.make_async_copy(source, target, load_sem.at[2 * counts[0] + n]))
    for load in loads:
        load.start()

    barrier = pltpu.get_barrier_semaphore()
    rank = (here[0] * sizes[1] + here[1]) * sizes[2] + here[2]

    def greet(step, carry):
        other = lax.rem(rank + step, devices)
        place = {
            "gx": other // (sizes[1] * sizes[2]),
            "gy": lax.rem(other // sizes[2], sizes[1]),
            "gz": lax.rem(other, sizes[2]),
        }
        pl.semaphore_signal(barrier, inc=1, device_id=place, device_id_type=MESH)
        return carry

    lax.fori_loop(1, devices, greet, 0)

    order = cell_order(counts[1], counts[2])

    def take_in(a):
        for source, load, start in ((tok_ref, loads[2 * a], 0), (upw_ref, loads[2 * a + 1], width)):
            load.wait()
            for x in range(SHIFT):
                moved = dot(order, source[a * SHIFT + x].reshape(plane, width)).astype(half)
                cells_ref[a, :, x * area : (x + 1) * area, start : start + width] = moved.reshape(
                    -1, area, width
                )

    arriving = {}
    for a in range(counts[0]):
        for b in range(counts[1]):
            for c in range(counts[2]):
                offset = tuple(int(at == 0) for at in (a, b, c))
                to = [(at - 1) % count for at, count in zip((a, b, c), counts)]
                window = (to[0] // 2 * spread[1] + to[1] // 2) * spread[2] + to[2] // 2
                octant = (to[0] % 2 * 2 + to[1] % 2) * 2 + to[2] % 2
                number = window * 8 + octant
                source = cells_ref.at[a, b * counts[2] + c]
                target = wins_ref.at[window, octant]
                if any(offset):
                    copy = pltpu.make_async_remote_copy(
                        src_ref=source,
                        dst_ref=target,
                        send_sem=send_sem.at[number],
                        recv_sem=recv_sem.at[number],
                        device_id={
                            axis: wrapped(at - step, size)
                            for axis, at, step, size in zip(axes, here, offset, sizes)
                        },
                        device_id_type=MESH,
                    )
                else:
                    copy = pltpu.make_async_copy(source, target, local_sem.at[number])
                arriving[number] = (copy, any(offset))

    def send(window, remote):
        for octant in range(8):
            copy, far = arriving[window * 8 + octant]
            if far == remote:
                copy.start()

    take_in(0)
    pl.semaphore_wait(barrier, devices - 1)
    early = counts[0] == 2 and min(counts[1:]) > 2
    if early:
        send(0, True)
    for a in range(1, counts[0]):
        take_in(a)
    if not early:
        send(0, True)
    send(0, False)
    qb_ref[...] = jnp.broadcast_to(qbias_ref[...], (8, 3 * width)).T[:, :1]
    loads[-2].wait()
    loads[-1].wait()
    wt_ref[...] = w_ref[...].T
    hid_ref[...] = jnp.ones_like(hid_ref)
    accq_ref[...] = jnp.zeros_like(accq_ref)
    accp_ref[...] = jnp.zeros_like(accp_ref)
    accs_ref[...] = jnp.zeros_like(accs_ref)
    tile = min(256, length)
    exponent = factor * 1.4426950408889634

    def one_window(step, nothing):
        for window in range(cells // 8):

            @pl.when(step == window)
            def _():
                for octant in range(8):
                    copy, remote = arriving[window * 8 + octant]
                    if remote:
                        copy.wait_recv()
                    else:
                        copy.wait()
                for later in {0: (1, 2)}.get(window, (window + 2,)):
                    if later < cells // 8:
                        send(later, True)
                        send(later, False)

        both = wins_ref[step].reshape(length, 2 * width)
        inputs = both[:, :width].astype(single)
        up = both[:, width:]
        centred = inputs - jnp.mean(inputs, axis=-1, keepdims=True)
        inverse = lax.rsqrt(jnp.mean(centred * centred, axis=-1, keepdims=True) + 1e-05)
        normed = centred * inverse
        normed_ref[...] = normed
        inv_ref[...] = inverse
        hidden = (normed * gain_ref[...] + nbias_ref[...]).astype(half)
        hid_ref[:, :width] = hidden
        pk_ref[...] = (dot_nt(wt_ref[...], hidden) + qb_ref[...]).astype(half)
        da_ref[...] = dot_nt(pw_ref[...], up).astype(half)

        place = (step // (spread[1] * spread[2]), step // spread[2] % spread[1], step % spread[2])
        cut = [
            jnp.where((at == size - 1) & (mine == count - 1), 1, 0)
            for at, size, mine, count in zip(here, sizes, place, spread)
        ]
        octants = lax.broadcasted_iota(jnp.int32, (16, length), 1) // CELL
        region = octants & (cut[0] * 4 + cut[1] * 2 + cut[2])
        own = region == lax.broadcasted_iota(jnp.int32, (16, length), 0)
        mark_q = jnp.where(own, 1.0, 0.0).astype(half)
        mark_k = jnp.where(own, 0.0, MASKED).astype(half)

        def one_head(h, carry):
            base = pl.multiple_of(h * head, head)
            qt = pk_ref[pl.ds(base, head), :]
            kt = pk_ref[pl.ds(base + width, head), :]
            vt = pk_ref[pl.ds(base + 2 * width, head), :]
            dat = da_ref[pl.ds(base, head), :]
            qt_marked = jnp.concatenate([qt, mark_q], axis=0)
            keys = jnp.concatenate([kt, mark_k], axis=0).T
            values = vt.T
            kg = jnp.zeros((head, length), single)
            vg = jnp.zeros((head, length), single)
            for start in range(0, length, tile):
                part = slice(start, start + tile)
                slot = start // tile % 2
                strips = [slice(at, at + STRIP) for at in range(0, length, STRIP)]
                peak = jnp.full((1, tile), 2 * MASKED, single)
                for strip in strips:
                    scores = dot(keys[strip], qt_marked[:, part])
                    s_ref[slot, strip, :] = scores
                    peak = jnp.maximum(peak, jnp.max(scores, axis=0, keepdims=True))
                norm = jnp.zeros((1, tile), single)
                inner = jnp.zeros((1, tile), single)
                for strip in strips:
                    prob_grad = dot(values[strip], dat[:, part])
                    expo = jnp.exp2((s_ref[slot, strip, :] - peak) * exponent)
                    norm += jnp.sum(expo, axis=0, keepdims=True)
                    inner += jnp.sum(expo * prob_grad, axis=0, keepdims=True)
                    s_ref[slot, strip, :] = expo
                    d_ref[slot, strip, :] = prob_grad
                share = 1.0 / norm
                inner = inner * share
                for strip in strips:
                    probs = s_ref[slot, strip, :] * share
                    ph_ref[slot, strip, :] = probs.astype(half)
                    ds_ref[slot, strip, :] = (probs * (d_ref[slot, strip, :] - inner)).astype(half)
                probs_half = ph_ref[slot]
                score_grad = ds_ref[slot]
                att_ref[pl.ds(base, head), part] = dot(vt, probs_half).astype(half)
                pg_ref[pl.ds(base, head), part] = (dot(kt, score_grad) * factor).astype(half)
                vg += dot_nt(dat[:, part], probs_half)
                kg += dot_nt(qt[:, part], score_grad)
            pg_ref[pl.ds(base + width, head), :] = (kg * factor).astype(half)
            pg_ref[pl.ds(base + 2 * width, head), :] = vg.astype(half)
            return carry

        lax.fori_loop(0, HEADS, one_head, 0, unroll=6)

        accq_ref[...] += dot(pg_ref[...], hid_ref[...])
        accp_ref[...] += dot(att_ref[...], up)
        hidden_grad = dot(w_ref[...], pg_ref[...]).T
        normed = normed_ref[...]
        up_single = up.astype(single)
        accs_ref[0:1, :] += jnp.sum(up_single, axis=0, keepdims=True)
        accs_ref[1:2, :] += jnp.sum(hidden_grad * normed, axis=0, keepdims=True)
        accs_ref[2:3, :] += jnp.sum(hidden_grad, axis=0, keepdims=True)
        normed_grad = hidden_grad * gain_ref[...]
        first = jnp.mean(normed_grad, axis=-1, keepdims=True)
        second = jnp.mean(normed_grad * normed, axis=-1, keepdims=True)
        token_grad = up_single + inv_ref[...] * (normed_grad - first - normed * second)
        res_ref[step] = token_grad.astype(half).reshape(8, CELL, width)
        return nothing

    lax.fori_loop(0, cells // 8, one_window, 0)

    total_rows = g_ref.shape[0]
    rest = width - LANES
    low = 4 * width
    last = slice(low + 3 * width, 2 * low)
    if total_rows > 2 * low:
        g_ref[2 * low :, :] = jnp.zeros((total_rows - 2 * low, LANES), single)
    g_ref[: 3 * width, :] = accq_ref[:, :LANES]
    g_ref[3 * width : low, :] = accp_ref[:, :LANES]
    g_ref[low : low + 3 * width, :] = accq_ref[:, LANES:]
    g_ref[last, :] = jnp.zeros((width, LANES), single)
    g_ref[last, :rest] = accp_ref[:, LANES:]
    g_ref[last, rest : rest + 8] = accs_ref[...].T

    middle = total_rows // 2
    chunk = middle // chips
    pair = {"gy": 1 - core}

    def chip(step):
        other = lax.rem(me + step, chips)
        return other, {"gx": other // sizes[2], "gz": lax.rem(other, sizes[2])}

    first_ref[...] = (g_ref[rows_at((1 - core) * middle, middle), :] * scale).astype(half)
    swap = pltpu.make_async_remote_copy(
        src_ref=first_ref, dst_ref=got_ref, send_sem=pair_send.at[0], recv_sem=pair_recv.at[0],
        device_id=pair, device_id_type=MESH,
    )
    swap.start()
    for number in sorted(arriving):
        if arriving[number][1]:
            arriving[number][0].wait_send()
    swap.wait()
    mine_ref[...] = (
        g_ref[rows_at(core * middle, middle), :] * scale + got_ref[...].astype(single)
    ).astype(half)

    def scatter(step):
        other, device = chip(step)
        return pltpu.make_async_remote_copy(
            src_ref=mine_ref.at[rows_at(other * chunk, chunk), :],
            dst_ref=parts_ref.at[step],
            send_sem=send2.at[step], recv_sem=recv2.at[step],
            device_id=device, device_id_type=MESH,
        )

    def start_scatter(step, carry):
        scatter(step).start()
        return carry

    def wait_scatter(step, carry):
        scatter(step).wait()
        return carry

    lax.fori_loop(1, chips, start_scatter, 0)

    def put_back(first_x, last_x):
        for x in range(first_x, last_x):
            inside = slice(x % SHIFT * area, (x % SHIFT + 1) * area)
            pieces = []
            for b in range(counts[1]):
                for c in range(counts[2]):
                    a = x // SHIFT
                    window = (a // 2 * spread[1] + b // 2) * spread[2] + c // 2
                    octant = (a % 2 * 2 + b % 2) * 2 + c % 2
                    pieces.append(res_ref[window, octant, inside, :])
            moved = lax.dot_general(
                order, jnp.concatenate(pieces, axis=0), (((0,), (0,)), ((), ())),
                preferred_element_type=single,
            )
            out_ref[x] = moved.astype(half).reshape(out_ref.shape[1:])

    planes = counts[0] * SHIFT
    put_back(0, planes // 2)
    lax.fori_loop(1, chips, wait_scatter, 0)
    parts_ref[0] = mine_ref[rows_at(me * chunk, chunk), :]
    spot = rows_at(core * middle + me * chunk, chunk)

    def add(step, total):
        return total + parts_ref[step].astype(single)

    total = lax.fori_loop(0, chips, add, jnp.zeros((chunk, LANES), single))
    tot_ref[spot, :] = total.astype(half)

    def gather(step):
        return pltpu.make_async_remote_copy(
            src_ref=tot_ref.at[spot, :],
            dst_ref=tot_ref.at[spot, :],
            send_sem=send3.at[step], recv_sem=recv3.at[step],
            device_id=chip(step)[1], device_id_type=MESH,
        )

    def start_gather(step, carry):
        gather(step).start()
        return carry

    def wait_gather(step, carry):
        gather(step).wait()
        return carry

    lax.fori_loop(1, chips, start_gather, 0)
    put_back(planes // 2, planes)
    lax.fori_loop(1, chips, wait_gather, 0)
    final = rows_at(core * middle, middle)
    swap = pltpu.make_async_remote_copy(
        src_ref=tot_ref.at[final, :], dst_ref=tot_ref.at[final, :],
        send_sem=pair_send.at[1], recv_sem=pair_recv.at[1],
        device_id=pair, device_id_type=MESH,
    )
    swap.start()
    swap.wait()
    qgrad_ref[:LANES, :] = tot_ref[: 3 * width, :].astype(single).T
    high = tot_ref[low : low + 3 * width, :].astype(single).T
    qgrad_ref[LANES:, :] = high[:rest]
    qbgrad_ref[...] = high[rest : rest + 1]
    ends = tot_ref[last, :].astype(single)
    pgrad_ref[:, :LANES] = tot_ref[3 * width : low, :].astype(single)
    pgrad_ref[:, LANES:] = ends[:, :rest]
    small_ref[...] = ends.T[rest : rest + 8]


def per_device(tokens, upstream, norm_gain, norm_bias, qkv_weight, qkv_bias, proj_weight):
    x, y, z, width = tokens.shape
    chips = lax.axis_size("gx") * lax.axis_size("gz")
    devices = chips * lax.axis_size("gy")
    counts = (x // SHIFT, y // SHIFT, z // SHIFT)
    cells = counts[0] * counts[1] * counts[2]
    length = WIN**3
    step = 16 * devices
    rows = -(-8 * width // step) * step
    middle = rows // 2
    scale = float(x * y * z * devices) ** (-0.5)
    vmem = pl.BlockSpec(memory_space=pltpu.VMEM)
    hbm = pl.BlockSpec(memory_space=pltpu.HBM)
    half = jnp.bfloat16
    single = jnp.float32
    dma = pltpu.SemaphoreType.DMA
    token_grad, qgrad, qbgrad, pgrad, small = pl.pallas_call(
        functools.partial(kernel, counts, width, scale),
        out_shape=(
            jax.ShapeDtypeStruct(tokens.shape, half),
            jax.ShapeDtypeStruct((width, 3 * width), single),
            jax.ShapeDtypeStruct((1, 3 * width), single),
            jax.ShapeDtypeStruct((width, width), single),
            jax.ShapeDtypeStruct((8, width), single),
        ),
        in_specs=[hbm, hbm, vmem, vmem, hbm, vmem, hbm],
        out_specs=(vmem,) * 5,
        scratch_shapes=[
            pltpu.VMEM(tokens.shape, half),
            pltpu.VMEM(tokens.shape, half),
            pltpu.VMEM((width, 3 * width), half),
            pltpu.VMEM((width, width), half),
            pltpu.VMEM((3 * width, width), half),
            pltpu.VMEM((counts[0], counts[1] * counts[2], CELL, 2 * width), half),
            pltpu.VMEM((cells // 8, 8, CELL, 2 * width), half),
            pltpu.VMEM((cells // 8, 8, CELL, width), half),
            pltpu.VMEM((length, 2 * LANES), half),
            pltpu.VMEM((length, width), single),
            pltpu.VMEM((length, 1), single),
            pltpu.VMEM((3 * width, length), half),
            pltpu.VMEM((width, length), half),
            pltpu.VMEM((width, length), half),
            pltpu.VMEM((3 * width, length), half),
            pltpu.VMEM((3 * width, 2 * LANES), single),
            pltpu.VMEM((width, width), single),
            pltpu.VMEM((8, width), single),
            pltpu.VMEM((2, length, min(256, length)), single),
            pltpu.VMEM((2, length, min(256, length)), single),
            pltpu.VMEM((2, length, min(256, length)), half),
            pltpu.VMEM((2, length, min(256, length)), half),
            pltpu.VMEM((3 * width, 1), single),
            pltpu.VMEM((rows, LANES), single),
            pltpu.VMEM((rows, LANES), half),
            pltpu.VMEM((middle, LANES), half),
            pltpu.VMEM((middle, LANES), half),
            pltpu.VMEM((middle, LANES), half),
            pltpu.VMEM((chips, middle // chips, LANES), half),
            dma((2 * counts[0] + 2,)),
            dma((cells,)),
            dma((cells,)),
            dma((cells,)),
            dma((2,)),
            dma((2,)),
            dma((chips,)),
            dma((chips,)),
            dma((chips,)),
            dma((chips,)),
        ],
        compiler_params=pltpu.CompilerParams(
            collective_id=0, has_side_effects=True, vmem_limit_bytes=63 * 1024 * 1024
        ),
    )(
        tokens,
        upstream,
        norm_gain.reshape(1, width),
        norm_bias.reshape(1, width),
        qkv_weight,
        qkv_bias.reshape(1, 3 * width),
        proj_weight,
    )
    return (token_grad, qgrad, qbgrad[0], pgrad, small[0], small[1], small[2])


def solution(mesh):
    placed = (P("gx", "gy", "gz", None), P("gx", "gy", "gz", None), P(), P(), P(), P(), P())
    return jax.shard_map(
        per_device,
        mesh=mesh,
        in_specs=placed,
        out_specs=(P("gx", "gy", "gz", None), P(), P(), P(), P(), P(), P()),
        check_vma=False,
    )
```

```python
import functools

import jax
import jax.numpy as jnp
from jax import lax
from jax.experimental import pallas as pl
from jax.experimental.pallas import tpu as pltpu
from jax.sharding import PartitionSpec as P

HEADS = 6
WIN = 8
SHIFT = 4
CELL = SHIFT**3
LANES = 128
STRIP = 128
MASKED = -1e30
MESH = pl.DeviceIdType.MESH


def dot(left, right):
    return jnp.dot(left, right, preferred_element_type=jnp.float32)


def dot_nt(left, right):
    return lax.dot_general(
        left, right, (((1,), (1,)), ((), ())), preferred_element_type=jnp.float32
    )


def wrapped(value, size):
    return lax.rem(value + size, size)


def rows_at(start, size):
    return pl.ds(pl.multiple_of(start, 16), size)


def cell_order(cells_y, cells_z):
    area = SHIFT * SHIFT
    count = cells_y * cells_z * area
    row = lax.broadcasted_iota(jnp.int32, (count, count), 0)
    column = lax.broadcasted_iota(jnp.int32, (count, count), 1)
    cell, inside = row // area, row % area
    y = cell // cells_z * SHIFT + inside // SHIFT
    z = cell % cells_z * SHIFT + inside % SHIFT
    return jnp.where(column == y * (cells_z * SHIFT) + z, 1.0, 0.0).astype(jnp.bfloat16)


def kernel(
    counts, width, scale, tok_hbm, upw_hbm, gain_ref, nbias_ref, w_hbm, qbias_ref, pw_hbm,
    out_ref, qgrad_ref, qbgrad_ref, pgrad_ref, small_ref,
    tok_ref, upw_ref, w_ref, pw_ref, wt_ref, cells_ref, wins_ref, res_ref, hid_ref, normed_ref, inv_ref, pk_ref, da_ref, att_ref, pg_ref,
    accq_ref, accp_ref, accs_ref, s_ref, d_ref, ph_ref, ds_ref, qb_ref, g_ref, tot_ref, first_ref, got_ref, mine_ref, parts_ref,
    load_sem, send_sem, recv_sem, local_sem, pair_send, pair_recv, send2, recv2, send3, recv3,
):
    axes = ("gx", "gy", "gz")
    here = [lax.axis_index(axis) for axis in axes]
    sizes = [lax.axis_size(axis) for axis in axes]
    devices = sizes[0] * sizes[1] * sizes[2]
    chips = sizes[0] * sizes[2]
    core = here[1]
    me = here[0] * sizes[2] + here[2]
    spread = [count // 2 for count in counts]
    cells = counts[0] * counts[1] * counts[2]
    length = WIN**3
    area = SHIFT * SHIFT
    plane = counts[1] * counts[2] * area
    head = width // HEADS
    factor = head ** (-0.5)
    single = jnp.float32
    half = jnp.bfloat16

    loads = []
    for a in range(counts[0]):
        planes = pl.ds(a * SHIFT, SHIFT)
        for n, (source, target) in enumerate(((tok_hbm, tok_ref), (upw_hbm, upw_ref))):
            loads.append(
                pltpu.make_async_copy(
                    source.at[planes], target.at[planes], load_sem.at[2 * a + n]
                )
            )
    for n, (source, target) in enumerate(((w_hbm, w_ref), (pw_hbm, pw_ref))):
        loads.append(pltpu.make_async_copy(source, target, load_sem.at[2 * counts[0] + n]))
    for load in loads:
        load.start()

    barrier = pltpu.get_barrier_semaphore()
    rank = (here[0] * sizes[1] + here[1]) * sizes[2] + here[2]

    def greet(step, carry):
        other = lax.rem(rank + step, devices)
        place = {
            "gx": other // (sizes[1] * sizes[2]),
            "gy": lax.rem(other // sizes[2], sizes[1]),
            "gz": lax.rem(other, sizes[2]),
        }
        pl.semaphore_signal(barrier, inc=1, device_id=place, device_id_type=MESH)
        return carry

    lax.fori_loop(1, devices, greet, 0)

    order = cell_order(counts[1], counts[2])

    def take_in(a):
        for source, load, start in ((tok_ref, loads[2 * a], 0), (upw_ref, loads[2 * a + 1], width)):
            load.wait()
            for x in range(SHIFT):
                moved = dot(order, source[a * SHIFT + x].reshape(plane, width)).astype(half)
                cells_ref[a, :, x * area : (x + 1) * area, start : start + width] = moved.reshape(
                    -1, area, width
                )

    arriving = {}
    for a in range(counts[0]):
        for b in range(counts[1]):
            for c in range(counts[2]):
                offset = tuple(int(at == 0) for at in (a, b, c))
                to = [(at - 1) % count for at, count in zip((a, b, c), counts)]
                window = (to[0] // 2 * spread[1] + to[1] // 2) * spread[2] + to[2] // 2
                octant = (to[0] % 2 * 2 + to[1] % 2) * 2 + to[2] % 2
                number = window * 8 + octant
                source = cells_ref.at[a, b * counts[2] + c]
                target = wins_ref.at[window, octant]
                if any(offset):
                    copy = pltpu.make_async_remote_copy(
                        src_ref=source,
                        dst_ref=target,
                        send_sem=send_sem.at[number],
                        recv_sem=recv_sem.at[number],
                        device_id={
                            axis: wrapped(at - step, size)
                            for axis, at, step, size in zip(axes, here, offset, sizes)
                        },
                        device_id_type=MESH,
                    )
                else:
                    copy = pltpu.make_async_copy(source, target, local_sem.at[number])
                arriving[number] = (copy, any(offset))

    def send(window, remote):
        for octant in range(8):
            copy, far = arriving[window * 8 + octant]
            if far == remote:
                copy.start()

    take_in(0)
    pl.semaphore_wait(barrier, devices - 1)
    early = counts[0] == 2 and min(counts[1:]) > 2
    if early:
        send(0, True)
    for a in range(1, counts[0]):
        take_in(a)
    if not early:
        send(0, True)
    send(0, False)
    qb_ref[...] = jnp.broadcast_to(qbias_ref[...], (8, 3 * width)).T[:, :1]
    loads[-2].wait()
    loads[-1].wait()
    wt_ref[...] = w_ref[...].T
    hid_ref[...] = jnp.ones_like(hid_ref)
    accq_ref[...] = jnp.zeros_like(accq_ref)
    accp_ref[...] = jnp.zeros_like(accp_ref)
    accs_ref[...] = jnp.zeros_like(accs_ref)
    tile = min(256, length)
    exponent = factor * 1.4426950408889634

    def one_window(step, nothing):
        for window in range(cells // 8):

            @pl.when(step == window)
            def _():
                for octant in range(8):
                    copy, remote = arriving[window * 8 + octant]
                    if remote:
                        copy.wait_recv()
                    else:
                        copy.wait()
                for later in {0: (1, 2)}.get(window, (window + 2,)):
                    if later < cells // 8:
                        send(later, True)
                        send(later, False)

        both = wins_ref[step].reshape(length, 2 * width)
        inputs = both[:, :width].astype(single)
        up = both[:, width:]
        centred = inputs - jnp.mean(inputs, axis=-1, keepdims=True)
        inverse = lax.rsqrt(jnp.mean(centred * centred, axis=-1, keepdims=True) + 1e-05)
        normed = centred * inverse
        normed_ref[...] = normed
        inv_ref[...] = inverse
        hidden = (normed * gain_ref[...] + nbias_ref[...]).astype(half)
        hid_ref[:, :width] = hidden
        pk_ref[...] = (dot_nt(wt_ref[...], hidden) + qb_ref[...]).astype(half)
        da_ref[...] = dot_nt(pw_ref[...], up).astype(half)

        place = (step // (spread[1] * spread[2]), step // spread[2] % spread[1], step % spread[2])
        cut = [
            jnp.where((at == size - 1) & (mine == count - 1), 1, 0)
            for at, size, mine, count in zip(here, sizes, place, spread)
        ]
        octants = lax.broadcasted_iota(jnp.int32, (16, length), 1) // CELL
        region = octants & (cut[0] * 4 + cut[1] * 2 + cut[2])
        own = region == lax.broadcasted_iota(jnp.int32, (16, length), 0)
        mark_q = jnp.where(own, 1.0, 0.0).astype(half)
        mark_k = jnp.where(own, 0.0, MASKED).astype(half)

        def one_head(h, carry):
            base = pl.multiple_of(h * head, head)
            qt = pk_ref[pl.ds(base, head), :]
            kt = pk_ref[pl.ds(base + width, head), :]
            vt = pk_ref[pl.ds(base + 2 * width, head), :]
            dat = da_ref[pl.ds(base, head), :]
            qt_marked = jnp.concatenate([qt, mark_q], axis=0)
            keys = jnp.concatenate([kt, mark_k], axis=0).T
            values = vt.T
            kg = jnp.zeros((head, length), single)
            vg = jnp.zeros((head, length), single)
            for start in range(0, length, tile):
                part = slice(start, start + tile)
                slot = start // tile % 2
                strips = [slice(at, at + STRIP) for at in range(0, length, STRIP)]
                peak = jnp.full((1, tile), 2 * MASKED, single)
                for strip in strips:
                    scores = dot(keys[strip], qt_marked[:, part])
                    s_ref[slot, strip, :] = scores
                    peak = jnp.maximum(peak, jnp.max(scores, axis=0, keepdims=True))
                norm = jnp.zeros((1, tile), single)
                inner = jnp.zeros((1, tile), single)
                for strip in strips:
                    prob_grad = dot(values[strip], dat[:, part])
                    expo = jnp.exp2((s_ref[slot, strip, :] - peak) * exponent)
                    norm += jnp.sum(expo, axis=0, keepdims=True)
                    inner += jnp.sum(expo * prob_grad, axis=0, keepdims=True)
                    s_ref[slot, strip, :] = expo
                    d_ref[slot, strip, :] = prob_grad
                share = 1.0 / norm
                inner = inner * share
                for strip in strips:
                    probs = s_ref[slot, strip, :] * share
                    ph_ref[slot, strip, :] = probs.astype(half)
                    ds_ref[slot, strip, :] = (probs * (d_ref[slot, strip, :] - inner)).astype(half)
                probs_half = ph_ref[slot]
                score_grad = ds_ref[slot]
                att_ref[pl.ds(base, head), part] = dot(vt, probs_half).astype(half)
                pg_ref[pl.ds(base, head), part] = (dot(kt, score_grad) * factor).astype(half)
                vg += dot_nt(dat[:, part], probs_half)
                kg += dot_nt(qt[:, part], score_grad)
            pg_ref[pl.ds(base + width, head), :] = (kg * factor).astype(half)
            pg_ref[pl.ds(base + 2 * width, head), :] = vg.astype(half)
            return carry

        lax.fori_loop(0, HEADS, one_head, 0, unroll=6)

        accq_ref[...] += dot(pg_ref[...], hid_ref[...])
        accp_ref[...] += dot(att_ref[...], up)
        hidden_grad = dot(w_ref[...], pg_ref[...]).T
        normed = normed_ref[...]
        up_single = up.astype(single)
        accs_ref[0:1, :] += jnp.sum(up_single, axis=0, keepdims=True)
        accs_ref[1:2, :] += jnp.sum(hidden_grad * normed, axis=0, keepdims=True)
        accs_ref[2:3, :] += jnp.sum(hidden_grad, axis=0, keepdims=True)
        normed_grad = hidden_grad * gain_ref[...]
        first = jnp.mean(normed_grad, axis=-1, keepdims=True)
        second = jnp.mean(normed_grad * normed, axis=-1, keepdims=True)
        token_grad = up_single + inv_ref[...] * (normed_grad - first - normed * second)
        res_ref[step] = token_grad.astype(half).reshape(8, CELL, width)
        return nothing

    lax.fori_loop(0, cells // 8, one_window, 0)

    total_rows = g_ref.shape[0]
    rest = width - LANES
    low = 4 * width
    last = slice(low + 3 * width, 2 * low)
    if total_rows > 2 * low:
        g_ref[2 * low :, :] = jnp.zeros((total_rows - 2 * low, LANES), single)
    g_ref[: 3 * width, :] = accq_ref[:, :LANES]
    g_ref[3 * width : low, :] = accp_ref[:, :LANES]
    g_ref[low : low + 3 * width, :] = accq_ref[:, LANES:]
    g_ref[last, :] = jnp.zeros((width, LANES), single)
    g_ref[last, :rest] = accp_ref[:, LANES:]
    g_ref[last, rest : rest + 8] = accs_ref[...].T

    middle = total_rows // 2
    chunk = middle // chips
    pair = {"gy": 1 - core}

    def chip(step):
        other = lax.rem(me + step, chips)
        return other, {"gx": other // sizes[2], "gz": lax.rem(other, sizes[2])}

    first_ref[...] = (g_ref[rows_at((1 - core) * middle, middle), :] * scale).astype(half)
    swap = pltpu.make_async_remote_copy(
        src_ref=first_ref, dst_ref=got_ref, send_sem=pair_send.at[0], recv_sem=pair_recv.at[0],
        device_id=pair, device_id_type=MESH,
    )
    swap.start()
    for number in sorted(arriving):
        if arriving[number][1]:
            arriving[number][0].wait_send()
    swap.wait()
    mine_ref[...] = (
        g_ref[rows_at(core * middle, middle), :] * scale + got_ref[...].astype(single)
    ).astype(half)

    def scatter(step):
        other, device = chip(step)
        return pltpu.make_async_remote_copy(
            src_ref=mine_ref.at[rows_at(other * chunk, chunk), :],
            dst_ref=parts_ref.at[step],
            send_sem=send2.at[step], recv_sem=recv2.at[step],
            device_id=device, device_id_type=MESH,
        )

    def start_scatter(step, carry):
        scatter(step).start()
        return carry

    def wait_scatter(step, carry):
        scatter(step).wait()
        return carry

    lax.fori_loop(1, chips, start_scatter, 0)

    def put_back(first_x, last_x):
        for x in range(first_x, last_x):
            inside = slice(x % SHIFT * area, (x % SHIFT + 1) * area)
            pieces = []
            for b in range(counts[1]):
                for c in range(counts[2]):
                    a = x // SHIFT
                    window = (a // 2 * spread[1] + b // 2) * spread[2] + c // 2
                    octant = (a % 2 * 2 + b % 2) * 2 + c % 2
                    pieces.append(res_ref[window, octant, inside, :])
            moved = lax.dot_general(
                order, jnp.concatenate(pieces, axis=0), (((0,), (0,)), ((), ())),
                preferred_element_type=single,
            )
            out_ref[x] = moved.astype(half).reshape(out_ref.shape[1:])

    planes = counts[0] * SHIFT
    put_back(0, planes // 2)
    lax.fori_loop(1, chips, wait_scatter, 0)
    parts_ref[0] = mine_ref[rows_at(me * chunk, chunk), :]
    spot = rows_at(core * middle + me * chunk, chunk)

    def add(step, total):
        return total + parts_ref[step].astype(single)

    total = lax.fori_loop(0, chips, add, jnp.zeros((chunk, LANES), single))
    tot_ref[spot, :] = total.astype(half)

    def gather(step):
        return pltpu.make_async_remote_copy(
            src_ref=tot_ref.at[spot, :],
            dst_ref=tot_ref.at[spot, :],
            send_sem=send3.at[step], recv_sem=recv3.at[step],
            device_id=chip(step)[1], device_id_type=MESH,
        )

    def start_gather(step, carry):
        gather(step).start()
        return carry

    def wait_gather(step, carry):
        gather(step).wait()
        return carry

    lax.fori_loop(1, chips, start_gather, 0)
    put_back(planes // 2, planes)
    lax.fori_loop(1, chips, wait_gather, 0)
    final = rows_at(core * middle, middle)
    swap = pltpu.make_async_remote_copy(
        src_ref=tot_ref.at[final, :], dst_ref=tot_ref.at[final, :],
        send_sem=pair_send.at[1], recv_sem=pair_recv.at[1],
        device_id=pair, device_id_type=MESH,
    )
    swap.start()
    swap.wait()
    qgrad_ref[:LANES, :] = tot_ref[: 3 * width, :].astype(single).T
    high = tot_ref[low : low + 3 * width, :].astype(single).T
    qgrad_ref[LANES:, :] = high[:rest]
    qbgrad_ref[...] = high[rest : rest + 1]
    ends = tot_ref[last, :].astype(single)
    pgrad_ref[:, :LANES] = tot_ref[3 * width : low, :].astype(single)
    pgrad_ref[:, LANES:] = ends[:, :rest]
    small_ref[...] = ends.T[rest : rest + 8]


def per_device(tokens, upstream, norm_gain, norm_bias, qkv_weight, qkv_bias, proj_weight):
    x, y, z, width = tokens.shape
    chips = lax.axis_size("gx") * lax.axis_size("gz")
    devices = chips * lax.axis_size("gy")
    counts = (x // SHIFT, y // SHIFT, z // SHIFT)
    cells = counts[0] * counts[1] * counts[2]
    length = WIN**3
    step = 16 * devices
    rows = -(-8 * width // step) * step
    middle = rows // 2
    scale = float(x * y * z * devices) ** (-0.5)
    vmem = pl.BlockSpec(memory_space=pltpu.VMEM)
    hbm = pl.BlockSpec(memory_space=pltpu.HBM)
    half = jnp.bfloat16
    single = jnp.float32
    dma = pltpu.SemaphoreType.DMA
    token_grad, qgrad, qbgrad, pgrad, small = pl.pallas_call(
        functools.partial(kernel, counts, width, scale),
        out_shape=(
            jax.ShapeDtypeStruct(tokens.shape, half),
            jax.ShapeDtypeStruct((width, 3 * width), single),
            jax.ShapeDtypeStruct((1, 3 * width), single),
            jax.ShapeDtypeStruct((width, width), single),
            jax.ShapeDtypeStruct((8, width), single),
        ),
        in_specs=[hbm, hbm, vmem, vmem, hbm, vmem, hbm],
        out_specs=(vmem,) * 5,
        scratch_shapes=[
            pltpu.VMEM(tokens.shape, half),
            pltpu.VMEM(tokens.shape, half),
            pltpu.VMEM((width, 3 * width), half),
            pltpu.VMEM((width, width), half),
            pltpu.VMEM((3 * width, width), half),
            pltpu.VMEM((counts[0], counts[1] * counts[2], CELL, 2 * width), half),
            pltpu.VMEM((cells // 8, 8, CELL, 2 * width), half),
            pltpu.VMEM((cells // 8, 8, CELL, width), half),
            pltpu.VMEM((length, 2 * LANES), half),
            pltpu.VMEM((length, width), single),
            pltpu.VMEM((length, 1), single),
            pltpu.VMEM((3 * width, length), half),
            pltpu.VMEM((width, length), half),
            pltpu.VMEM((width, length), half),
            pltpu.VMEM((3 * width, length), half),
            pltpu.VMEM((3 * width, 2 * LANES), single),
            pltpu.VMEM((width, width), single),
            pltpu.VMEM((8, width), single),
            pltpu.VMEM((2, length, min(256, length)), single),
            pltpu.VMEM((2, length, min(256, length)), single),
            pltpu.VMEM((2, length, min(256, length)), half),
            pltpu.VMEM((2, length, min(256, length)), half),
            pltpu.VMEM((3 * width, 1), single),
            pltpu.VMEM((rows, LANES), single),
            pltpu.VMEM((rows, LANES), half),
            pltpu.VMEM((middle, LANES), half),
            pltpu.VMEM((middle, LANES), half),
            pltpu.VMEM((middle, LANES), half),
            pltpu.VMEM((chips, middle // chips, LANES), half),
            dma((2 * counts[0] + 2,)),
            dma((cells,)),
            dma((cells,)),
            dma((cells,)),
            dma((2,)),
            dma((2,)),
            dma((chips,)),
            dma((chips,)),
            dma((chips,)),
            dma((chips,)),
        ],
        compiler_params=pltpu.CompilerParams(
            collective_id=0, has_side_effects=True, vmem_limit_bytes=48 * 1024 * 1024
        ),
    )(
        tokens,
        upstream,
        norm_gain.reshape(1, width),
        norm_bias.reshape(1, width),
        qkv_weight,
        qkv_bias.reshape(1, 3 * width),
        proj_weight,
    )
    return (token_grad, qgrad, qbgrad[0], pgrad, small[0], small[1], small[2])


def solution(mesh):
    placed = (P("gx", "gy", "gz", None), P("gx", "gy", "gz", None), P(), P(), P(), P(), P())
    return jax.shard_map(
        per_device,
        mesh=mesh,
        in_specs=placed,
        out_specs=(P("gx", "gy", "gz", None), P(), P(), P(), P(), P(), P()),
        check_vma=False,
    )
```
